32 devices in a mesh: row: 8 (over y, x, core), col: 4 (over z).
Axes of the slice: x: 2, y: 2, z: 4, core: 2. Of those that a mesh axis runs over, the one named last changes fastest.
Arguments:
- grad_out: bfloat16 [1024, 16384], P('col', 'row'), may hold values from -6 to 6
- gate_act: bfloat16 [1024, 26624], P('row', 'col'), may hold values from -8 to 8
- up_act: bfloat16 [1024, 26624], P('row', 'col'), may hold values from -6 to 6
- down_weight: bfloat16 [26624, 16384], P('col', 'row'), may hold values from -0.046875 to 0.046875
Outputs:
- grad_gate: bfloat16 [1024, 26624], P('row', 'col')
- grad_up: bfloat16 [1024, 26624], P('row', 'col')
- grad_down: bfloat16 [26624, 16384], P('col', 'row')
The draws below stay inside these ranges and needn't reach their ends.
All inputs are finite; a program needn't handle non-finite values.
Results may differ from the reference program's by a relative error of at most 0.0049.
Values may be sent and summed in bfloat16 or wider, within the bound.
No kernel may reach another device: no remote copies, remote signals or barrier semaphores. Data moves between devices by JAX's collectives and lax.ppermute only.
A program may use at most 448 MiB of HBM per device.

```python
import jax
import jax.numpy as jnp
from jax import lax

D = 16384
F = 26624
TOKENS = 1024


def strengthened(array, rng, source, target, shards_of, factor):
    def block_of(position):
        return (jnp.arange(array.shape[position]) // (array.shape[position] // shards_of)).reshape((-1,) + (1,) * (array.ndim - 1 - position))

    one_side = jax.random.permutation(rng, shards_of)[block_of(target)]
    other_side = (block_of(target) + shards_of // 2) % shards_of
    return jnp.where((block_of(source) == one_side) | (block_of(source) == other_side), factor * array, array)


def block_scale(rng, shape, pieces, least, largest):
    def one(axis_at, parts):
        draws = jax.random.uniform(jax.random.fold_in(jax.random.fold_in(rng, 6), axis_at), (parts,), jnp.float32, least / len(pieces), largest / len(pieces))
        return jnp.repeat(jnp.exp(draws), shape[axis_at] // parts).reshape((-1,) + (1,) * (len(shape) - axis_at - 1))

    gain = one(*pieces[0])
    for cut in pieces[1:]:
        gain = gain * one(*cut)
    return gain


def centred(key, dims, scale, reach, split=(), kind=jnp.bfloat16):
    factor_of = block_scale(key, dims, split, -0.22, 0.18) if split else 1.0
    array = jax.random.normal(key, dims, jnp.float32) * scale * factor_of
    return jnp.minimum(jnp.maximum(array, -reach), reach).astype(kind)


def heavy_noise(rng, extent, width, most, pieces, heavy, held_as=jnp.bfloat16):
    entries = width * jax.random.normal(rng, extent, jnp.float32)
    if pieces:
        entries = entries * block_scale(rng, extent, pieces, -0.22, 0.18)
    return jnp.clip(strengthened(entries, jax.random.fold_in(rng, 3), *heavy), -most, most).astype(held_as)


def setup_inputs(seed: int = 0) -> dict:
    streams_of = jax.random.split(jax.random.key(seed), 5)
    grad_out = heavy_noise(streams_of[0], (TOKENS, D), 1.0, 6.0, ((0, 4), (1, 8)), (1, 0, 8, 2.0))
    gate_act = centred(streams_of[1], (TOKENS, F), 1.5, 8.0, ((0, 8), (1, 4)))
    up_act = centred(streams_of[2], (TOKENS, F), 1.0, 6.0, ((0, 8), (1, 4)))
    down_weight = centred(streams_of[3], (F, D), D ** -0.5, 0.046875, ((0, 4), (1, 8)))
    return {"grad_out": grad_out, "gate_act": gate_act, "up_act": up_act, "down_weight": down_weight}


def reference(grad_out, gate_act, up_act, down_weight):
    gate_val = gate_act.astype(jnp.float32)
    up_val = up_act.astype(jnp.float32)
    sigmoid_g = jax.nn.sigmoid(gate_val)
    act_val = gate_val * sigmoid_g
    hidden = (act_val * up_val).astype(jnp.bfloat16)
    grad_hidden = lax.dot_general(grad_out, down_weight, (((1,), (1,)), ((), ())), preferred_element_type=jnp.float32)
    grad_gate = (grad_hidden * up_val * sigmoid_g * (1.0 + gate_val * (1.0 - sigmoid_g))).astype(jnp.bfloat16)
    grad_up = (grad_hidden * act_val).astype(jnp.bfloat16)
    grad_down = lax.dot_general(hidden, grad_out, (((0,), (0,)), ((), ())), preferred_element_type=jnp.float32).astype(jnp.bfloat16)
    return grad_gate, grad_up, grad_down
```

```python
import jax
import jax.numpy as jnp
from jax import lax
from jax.sharding import PartitionSpec as P

CHUNKS = 4


def local(grad_out, gate_act, up_act, down_weight):
    f32, bf16 = jnp.float32, jnp.bfloat16
    gate = gate_act.astype(f32)
    hidden = (gate * jax.nn.sigmoid(gate) * up_act.astype(f32)).astype(bf16)
    dy = lax.all_gather(grad_out, "col", axis=0, tiled=True)
    hidden = lax.all_gather(hidden, "row", axis=0, tiled=True)
    dy, hidden = lax.optimization_barrier((dy, hidden))
    width = down_weight.shape[0] // CHUNKS
    gate_parts, up_parts = [], []
    for k in range(CHUNKS):
        cut = slice(k * width, (k + 1) * width)
        part = lax.dot_general(
            dy, down_weight[cut], (((1,), (1,)), ((), ())), preferred_element_type=f32
        ).astype(bf16)
        grad_hidden = lax.psum_scatter(part, "row", scatter_dimension=0, tiled=True).astype(f32)
        g, u = gate_act[:, cut].astype(f32), up_act[:, cut].astype(f32)
        sig = jax.nn.sigmoid(g)
        gate_parts.append((grad_hidden * u * sig * (1.0 + g * (1.0 - sig))).astype(bf16))
        up_parts.append((grad_hidden * (g * sig)).astype(bf16))
    grad_down = lax.dot_general(
        hidden, dy, (((0,), (0,)), ((), ())), preferred_element_type=f32
    ).astype(bf16)
    return jnp.concatenate(gate_parts, 1), jnp.concatenate(up_parts, 1), grad_down


def solution(mesh):
    return jax.shard_map(
        local,
        mesh=mesh,
        in_specs=(P("col", "row"), P("row", "col"), P("row", "col"), P("col", "row")),
        out_specs=(P("row", "col"), P("row", "col"), P("col", "row")),
        check_vma=False,
    )
```

```python
import functools

import jax
import jax.numpy as jnp
from jax import lax
from jax.experimental import pallas as pl
from jax.experimental.pallas import tpu as pltpu
from jax.sharding import PartitionSpec as P

F32, BF16 = jnp.float32, jnp.bfloat16
VMEM_LIMIT = 40 * 1024 * 1024
CHUNKS = 4
UNIT = 256


def params():
    return pltpu.CompilerParams(vmem_limit_bytes=VMEM_LIMIT)


def divisor(extent, most, step):
    best = extent
    for size in range(step, most + 1, step):
        if extent % size == 0:
            best = size
    return best


def hidden_kernel(gate_ref, up_ref, out_ref):
    gate = gate_ref[...].astype(F32)
    hidden = gate * jax.nn.sigmoid(gate) * up_ref[...].astype(F32)
    out_ref[...] = jnp.transpose(hidden).astype(BF16)


def hidden_transposed(gate, up, half):
    tokens, width = gate.shape
    rows = width // 2
    step = divisor(rows, 1664, 128)
    first = half * (rows // step)
    spec = pl.BlockSpec((tokens, step), lambda i: (0, first + i))
    return pl.pallas_call(
        hidden_kernel,
        grid=(rows // step,),
        in_specs=[spec, spec],
        out_specs=pl.BlockSpec((step, tokens), lambda i: (i, 0)),
        out_shape=jax.ShapeDtypeStruct((rows, tokens), BF16),
        compiler_params=params(),
        cost_estimate=pl.CostEstimate(
            flops=10 * rows * tokens, bytes_accessed=6 * rows * tokens, transcendentals=rows * tokens
        ),
        name="hidden",
    )(gate, up)


def reorder_kernel(order_ref, in_ref, out_ref):
    out_ref[...] = in_ref[...]


def reorder(x, order, rows):
    depth = x.shape[1]
    grid_spec = pltpu.PrefetchScalarGridSpec(
        num_scalar_prefetch=1,
        grid=(x.shape[0] // rows,),
        in_specs=[pl.BlockSpec((rows, depth), lambda i, at: (at[i], 0))],
        out_specs=pl.BlockSpec((rows, depth), lambda i, at: (i, 0)),
    )
    return pl.pallas_call(
        reorder_kernel,
        grid_spec=grid_spec,
        out_shape=jax.ShapeDtypeStruct(x.shape, x.dtype),
        compiler_params=params(),
        cost_estimate=pl.CostEstimate(flops=0, bytes_accessed=4 * x.size, transcendentals=0),
        name="reorder",
    )(order, x)


def product_kernel(dy_ref, weight_ref, keep_ref, send_ref):
    half = keep_ref.shape[0]
    part = lax.dot_general(
        dy_ref[...], weight_ref[...], (((1,), (1,)), ((), ())), preferred_element_type=F32
    )
    keep_ref[...] = part[:half]
    send_ref[...] = part[half:].astype(BF16)


def hidden_grad_terms(dy, weight, first, tiles):
    tokens, depth = dy.shape
    half, width = tokens // 2, tiles * UNIT
    return pl.pallas_call(
        product_kernel,
        grid=(tiles,),
        in_specs=[
            pl.BlockSpec((tokens, depth), lambda i: (0, 0)),
            pl.BlockSpec((UNIT, depth), lambda i: (first + i, 0)),
        ],
        out_specs=[
            pl.BlockSpec((half, UNIT), lambda i: (0, i)),
            pl.BlockSpec((half, UNIT), lambda i: (0, i)),
        ],
        out_shape=[
            jax.ShapeDtypeStruct((half, width), F32),
            jax.ShapeDtypeStruct((half, width), BF16),
        ],
        compiler_params=params(),
        cost_estimate=pl.CostEstimate(
            flops=2 * tokens * depth * width,
            bytes_accessed=2 * (tokens * depth + depth * width) + 6 * half * width,
            transcendentals=0,
        ),
        name="hidden_grad_terms",
    )(dy, weight)


def weight_grad_kernel(pieces, *refs):
    dy_ref, out_ref = refs[pieces], refs[-1]
    hidden = jnp.concatenate([ref[...] for ref in refs[:pieces]], axis=1)
    out_ref[...] = jnp.dot(hidden, dy_ref[...], preferred_element_type=F32).astype(BF16)


def weight_grad(pieces, dy, whole, half):
    rows, block = pieces[0].shape
    tokens, depth = dy.shape
    tall = divisor(rows, 832, 16)
    wide = divisor(depth, 1024, 128)
    first = half * (rows // tall)
    n = len(pieces)
    in_specs = [pl.BlockSpec((tall, block), lambda i, k: (i, 0))] * n + [
        pl.BlockSpec((tokens, wide), lambda i, k: (0, k))
    ]
    args = list(pieces) + [dy]
    kernel = functools.partial(weight_grad_kernel, n)
    aliases = {}
    if whole is not None:
        in_specs.append(pl.BlockSpec(memory_space=pl.ANY))
        args.append(whole)
        aliases = {n + 1: 0}
    return pl.pallas_call(
        kernel,
        grid=(rows // tall, depth // wide),
        in_specs=in_specs,
        out_specs=pl.BlockSpec((tall, wide), lambda i, k: (first + i, k)),
        out_shape=jax.ShapeDtypeStruct((2 * rows, depth), BF16),
        input_output_aliases=aliases,
        compiler_params=params(),
        cost_estimate=pl.CostEstimate(
            flops=2 * rows * tokens * depth,
            bytes_accessed=2 * (rows * tokens + tokens * depth + rows * depth),
            transcendentals=0,
        ),
        name="weight_grad",
    )(*args)


def local(row_count, grad_out, gate_act, up_act, down_weight):
    me = lax.axis_index("row")
    bits = []
    while 2 ** (len(bits) + 1) < row_count:
        bits.append(2 ** (len(bits) + 1))
    streams = (bits, bits[::-1])
    width = down_weight.shape[0]
    block = gate_act.shape[0]

    def swap(x, bit):
        return lax.ppermute(x, "row", [(r, r ^ bit) for r in range(row_count)])

    def flips(order):
        found = [0]
        for bit in order[::-1] + [1]:
            found = found + [f | bit for f in found]
        return found

    dy = lax.all_gather(grad_out, "col", axis=0, tiled=True)

    gathered = []
    for half in range(2):
        held = {0: hidden_transposed(gate_act, up_act, half)}
        for bit in streams[half] + [1]:
            held.update({f | bit: swap(x, bit) for f, x in list(held.items())})
        gathered.append(held)

    dys = [
        reorder(dy, jnp.bitwise_xor(jnp.array(flips(s), jnp.int32), me.astype(jnp.int32)), block)
        for s in streams
    ]

    units = width // UNIT
    edges = [units * k // CHUNKS for k in range(CHUNKS + 1)]
    gate_parts, up_parts = [], []
    for k in range(CHUNKS):
        first, tiles = edges[k], edges[k + 1] - edges[k]
        stream = k % 2
        keep, send = hidden_grad_terms(dys[stream], down_weight, first, tiles)
        terms = [keep, swap(send, 1)]
        for bit in streams[stream]:
            rows = terms[0].shape[0] // 2
            send = sum(t[rows:].astype(F32) for t in terms).astype(BF16)
            terms = [t[:rows] for t in terms] + [swap(send, bit)]
        grad_hidden = sum(t.astype(F32) for t in terms)
        cut = slice(first * UNIT, (first + tiles) * UNIT)
        g, u = gate_act[:, cut].astype(F32), up_act[:, cut].astype(F32)
        sig = jax.nn.sigmoid(g)
        gate_parts.append((grad_hidden * u * sig * (1.0 + g * (1.0 - sig))).astype(BF16))
        up_parts.append((grad_hidden * (g * sig)).astype(BF16))

    grad_down = None
    for half in range(2):
        pieces = [gathered[half][f] for f in flips(streams[0])]
        grad_down = weight_grad(pieces, dys[0], grad_down, half)
    return jnp.concatenate(gate_parts, 1), jnp.concatenate(up_parts, 1), grad_down


def solution(mesh):
    return jax.shard_map(
        functools.partial(local, mesh.shape["row"]),
        mesh=mesh,
        in_specs=(P("col", "row"), P("row", "col"), P("row", "col"), P("col", "row")),
        out_specs=(P("row", "col"), P("row", "col"), P("col", "row")),
        check_vma=False,
    )
```

```python
import jax
import jax.numpy as jnp
from jax import lax
from jax.experimental import pallas as pl
from jax.experimental.pallas import tpu as pltpu
from jax.sharding import PartitionSpec as P

F32, BF16 = jnp.float32, jnp.bfloat16
VMEM_LIMIT = 63 * 1024 * 1024
CHUNKS = 4
PARTS = 4
UNIT = 256
PLAN = "P0 P1 S0 P2 S1 P3 S2 S3 W0 W1 S0 S1 W2 S2 S3 W3 F0 F1 F2 F3".split()


def divisor(extent, most, step):
    best = extent
    for size in range(step, most + 1, step):
        if extent % size == 0:
            best = size
    return best


def run(kernel, name, grid, ins, outs, deps=(), at=None, flops=0, exps=0):
    held = [(n, o[3]) for n, o in enumerate(outs) if o[3] is not None]
    deps = [d for d in deps if not any(d is x for _, x in held)]
    arrays = [x for x, _ in ins] + [x for _, x in held] + list(deps)
    specs = [s for _, s in ins] + [pl.BlockSpec(memory_space=pl.ANY)] * (len(held) + len(deps))
    lead = 0 if at is None else 1
    first_out = lead + len(arrays)

    def body(*refs):
        kernel(*refs[lead : lead + len(ins)], *refs[first_out:])

    moved = sum(x.size * x.dtype.itemsize for x, _ in ins)
    return pl.pallas_call(
        body,
        grid_spec=pltpu.PrefetchScalarGridSpec(
            num_scalar_prefetch=lead, grid=grid, in_specs=specs, out_specs=[o[2] for o in outs]
        ),
        out_shape=[jax.ShapeDtypeStruct(o[0], o[1]) for o in outs],
        input_output_aliases={lead + len(ins) + k: n for k, (n, _) in enumerate(held)},
        compiler_params=pltpu.CompilerParams(vmem_limit_bytes=VMEM_LIMIT),
        cost_estimate=pl.CostEstimate(flops=flops, bytes_accessed=moved, transcendentals=exps),
        name=name,
    )(*([] if at is None else [at]), *arrays)


def hidden_kernel(gate_ref, up_ref, out_ref):
    gate = gate_ref[...].astype(F32)
    hidden = gate * jax.nn.sigmoid(gate) * up_ref[...].astype(F32)
    out_ref[...] = jnp.transpose(hidden).astype(BF16)


def hidden_transposed(gate, up):
    tokens, width = gate.shape
    step = divisor(width, 1664, 128)
    spec = pl.BlockSpec((tokens, step), lambda i: (0, i))
    out = ((width, tokens), BF16, pl.BlockSpec((step, tokens), lambda i: (i, 0)), None)
    return run(hidden_kernel, "hidden", (width // step,), [(gate, spec), (up, spec)], [out])[0]


def product_kernel(mine_ref, other_ref, weight_ref, keep_ref, send_ref, *copy_ref):
    block = mine_ref.shape[0]
    dy = jnp.concatenate([mine_ref[...], other_ref[...]], axis=0)
    part = lax.dot_general(dy, weight_ref[...], (((1,), (1,)), ((), ())), preferred_element_type=F32)
    keep_ref[...] = part[:block]
    send_ref[...] = part[block:].astype(BF16)
    for ref in copy_ref:
        ref[...] = dy


def hidden_grad_terms(at, dy, weight, first, tiles, held, ordered, total, deps):
    block, depth = dy.shape[0] // 2, dy.shape[1]
    shape = (total // 2, tiles * UNIT)
    ins = [
        (dy, pl.BlockSpec((block, depth), lambda i, at: (at[1], 0))),
        (dy, pl.BlockSpec((block, depth), lambda i, at: (at[2], 0))),
        (weight, pl.BlockSpec((UNIT, depth), lambda i, at: (first + i, 0))),
    ]
    spec = pl.BlockSpec((block, UNIT), lambda i, at: (at[0], i))
    outs = [(shape, F32, spec, held[0]), (shape, BF16, spec, held[1])]
    if first == 0:
        copy = pl.BlockSpec((2 * block, depth), lambda i, at: (at[3], 0))
        outs.append(((total, depth), BF16, copy, ordered))
    flops = 4 * block * depth * tiles * UNIT
    return run(product_kernel, "hidden_grad_terms", (tiles,), ins, outs, deps, at, flops)


def stage_kernel(*refs):
    refs[-1][...] = sum(ref[...].astype(F32) for ref in refs[:-1]).astype(BF16)


def stage_sum(terms, rows, deps):
    width = terms[0].shape[1]
    steps = 2
    tall = rows // steps
    ins = [(t, pl.BlockSpec((tall, width), lambda i: (steps + i, 0))) for t in terms]
    out = ((rows, width), BF16, pl.BlockSpec((tall, width), lambda i: (i, 0)), None)
    return run(stage_kernel, "stage_sum", (steps,), ins, [out], deps)[0]


def finish_kernel(gate_ref, up_ref, *refs):
    grad_hidden = sum(ref[...].astype(F32) for ref in refs[:-2])
    gate, up = gate_ref[...].astype(F32), up_ref[...].astype(F32)
    sig = jax.nn.sigmoid(gate)
    refs[-2][...] = (grad_hidden * up * sig * (1.0 + gate * (1.0 - sig))).astype(BF16)
    refs[-1][...] = (grad_hidden * (gate * sig)).astype(BF16)


def finish(gate, up, terms, first, tiles, held, deps):
    tokens = gate.shape[0]
    width = tiles * UNIT
    window = pl.BlockSpec((pl.Element(tokens), pl.Element(width)), lambda i: (0, first * UNIT))
    ins = [(gate, window), (up, window)]
    ins += [(t, pl.BlockSpec((tokens, width), lambda i: (0, 0))) for t in terms]
    outs = [(gate.shape, BF16, window, x) for x in held]
    return run(finish_kernel, "finish", (1,), ins, outs, deps, exps=tokens * width)


def weight_grad_kernel(*refs):
    hidden = jnp.concatenate([ref[...] for ref in refs[:-2]], axis=1)
    refs[-1][...] = jnp.dot(hidden, refs[-2][...], preferred_element_type=F32).astype(BF16)


def weight_grad(pieces, dy, whole, total, start, rows, deps):
    block = pieces[0][0].shape[1]
    tokens, depth = dy.shape
    tall = divisor(rows, 416, 16)

    def spec(base):
        return pl.BlockSpec((tall, block), lambda i: ((start - base) // tall + i, 0))

    ins = [(x, spec(base)) for x, base in pieces]
    ins.append((dy, pl.BlockSpec((tokens, depth), lambda i: (0, 0))))
    out = ((total, depth), BF16, pl.BlockSpec((tall, depth), lambda i: (start // tall + i, 0)), whole)
    flops = 2 * rows * tokens * depth
    return run(weight_grad_kernel, "weight_grad", (rows // tall,), ins, [out], deps, flops=flops)[0]


def arrivals(z, count):
    found = []
    for s in range(1, count):
        if z - s >= 0:
            found.append(("up", s, z - s))
        if z + s < count:
            found.append(("down", s, z + s))
    return found


def pick(table, index):
    value = jnp.int32(table[0])
    for n in range(1, len(table)):
        value = jnp.where(index == n, jnp.int32(table[n]), value)
    return value


def program(row_count, col_count, grad_out, gate_act, up_act, down_weight):
    assert row_count == 2 * col_count
    row = lax.axis_index("row").astype(jnp.int32)
    col = lax.axis_index("col").astype(jnp.int32)
    core, chip = row % 2, row // 2
    bits = []
    while 2 ** (len(bits) + 1) < row_count:
        bits.append(2 ** (len(bits) + 1))
    streams = (bits, bits[::-1])
    width = down_weight.shape[0]
    block = gate_act.shape[0]
    tokens = row_count * block

    def swap(x, bit):
        pairs = [(r, r ^ bit) for r in range(row_count)]
        return jax.tree.map(lambda x: lax.ppermute(x, "row", pairs), x)

    places = []
    for order in streams:
        found = [0]
        for bit in order[::-1]:
            found = found + [f | bit // 2 for f in found]
        places.append([found.index(m) for m in range(row_count // 2)])

    ways = {"up": [grad_out], "down": [grad_out]}

    def forward(s):
        up, down = ways["up"], ways["down"]
        up.append(lax.ppermute(up[-1], "col", [(i, i + 1) for i in range(s - 1, col_count - 1)]))
        down.append(lax.ppermute(down[-1], "col", [(i, i - 1) for i in range(1, col_count - s + 1)]))

    def arrived(k):
        sources = [arrivals(z, col_count)[k - 1] for z in range(col_count)]
        value = None
        for z, (way, s, _) in enumerate(sources):
            x = ways[way][s]
            value = x if value is None else jnp.where(col == z, x, value)
        return value, pick([c for _, _, c in sources], col)

    units = width // UNIT
    edges = [units * k // CHUNKS for k in range(CHUNKS + 1)]
    terms = [(None, None)] * CHUNKS
    ordered = None

    def product(q, dy, source, deps):
        nonlocal ordered
        flip = chip ^ source
        at = jnp.stack([pick(places[q % 2], flip), core, 1 - core, flip])
        out = hidden_grad_terms(
            at, dy, down_weight, edges[q], edges[q + 1] - edges[q], terms[q], ordered, tokens, deps
        )
        terms[q] = tuple(out[:2])
        if q == 0:
            ordered = out[2]
        return out[0]

    forward(1)
    hidden = hidden_transposed(gate_act, up_act)
    held, base = {0: [hidden]}, {0: [0]}
    first_bits = bits[:2]
    for bit in first_bits + [1]:
        held[bit], base[bit] = swap([hidden], bit), [0]
    half = width // 2

    last = hidden
    early = {(1, 0): held[1]}
    dy, source = grad_out, col
    for k in range(col_count):
        for q in range(CHUNKS):
            if k == col_count - 1:
                break
            last = product(q, dy, source, [last] + early.pop((k, q), []))
        if k + 1 < col_count:
            ways["up"][k + 1], ways["down"][k + 1], last = lax.optimization_barrier(
                (ways["up"][k + 1], ways["down"][k + 1], last)
            )
            if k + 2 < col_count:
                forward(k + 2)
            dy, source = arrived(k + 1)
        if k == 1 and len(first_bits) == 2:
            a, b = first_bits
            held[a], held[b], held[1], dy, last = lax.optimization_barrier(
                (held[a], held[b], held[1], dy, last)
            )
            held[a | b] = [swap(held[a][0][:half], b), swap(held[b][0][half:], a)]
            base[a | b] = [0, half]
            both = swap(jnp.concatenate(held[a] + held[b]), 1)
            held[a | 1] = held[b | 1] = [both]
            base[a | 1], base[b | 1] = [0], [-width]
            early[k + 1, 1] = [both]

    held, last = lax.optimization_barrier((held, last))
    for bit in bits[2:]:
        for f in [f for f in held if f | bit not in held]:
            held[f | bit], base[f | bit] = swap(held[f], bit), base[f]
    ready = jax.tree.leaves(held)
    for f in [f for f in held if f | 1 not in held]:
        held[f | 1], base[f | 1] = swap(held[f], 1), base[f]

    grad_gate = grad_up = grad_down = None
    sums, stages = [None] * CHUNKS, [0] * CHUNKS
    part = width // PARTS

    def step(kind, n, last):
        nonlocal grad_gate, grad_up, grad_down
        if kind == "P":
            deps = ready if n == 0 else jax.tree.leaves(held) if n == 1 else []
            keep = product(n, dy, source, [last] + deps)
            sums[n] = [keep, swap(terms[n][1], 1)]
            return keep
        if kind == "S":
            bit = streams[n % 2][stages[n]]
            stages[n] += 1
            send = stage_sum(sums[n], (tokens // 2) >> stages[n], [last])
            sums[n] = sums[n] + [swap(send, bit)]
            return send
        if kind == "F":
            grad_gate, grad_up = finish(
                gate_act, up_act, sums[n], edges[n], edges[n + 1] - edges[n], (grad_gate, grad_up), [last]
            )
            return grad_up
        pieces = []
        for f in range(row_count):
            side = -1 if n * part >= half else 0
            pieces.append((held[f][side], base[f][side]))
        grad_down = weight_grad(pieces, ordered, grad_down, width, n * part, part, [last])
        return grad_down

    for item in PLAN:
        kind, n = item[0], int(item[1:])
        while kind == "F" and stages[n] < len(bits):
            last = step("S", n, last)
        last = step(kind, n, last)
    return grad_gate, grad_up, grad_down


def solution(mesh):
    def local(*args):
        return program(mesh.shape["row"], mesh.shape["col"], *args)

    return jax.shard_map(
        local,
        mesh=mesh,
        in_specs=(P("col", "row"), P("row", "col"), P("row", "col"), P("col", "row")),
        out_specs=(P("row", "col"), P("row", "col"), P("col", "row")),
        check_vma=False,
    )
```

```python
import functools
import math

import jax
import jax.numpy as jnp
from jax import lax
from jax.experimental import pallas as pl
from jax.experimental.pallas import tpu as pltpu
from jax.sharding import PartitionSpec as P

F32, BF16 = jnp.float32, jnp.bfloat16
VMEM_LIMIT = 63 * 1024 * 1024
CHUNKS = 4
GROUPS = 2
PARTS = 4
LANES = 128
PLAN = ["P0 P1 S0 S1", "S2 S3 W0 S0", "S1 W1 W2 S2", "S3 W3 F0 F1", "F2 F3"]


def divisor(extent, most, step):
    best = extent
    for size in range(step, most + 1, step):
        if extent % size == 0:
            best = size
    return best


def run(kernel, name, grid, ins, outs, deps=(), at=None, scratch=(), flops=0, exps=0):
    held = [(n, o[3]) for n, o in enumerate(outs) if o[3] is not None]
    deps = [d for d in deps if not any(d is x for _, x in held)]
    arrays = [x for x, _ in ins] + [x for _, x in held] + list(deps)
    specs = [s for _, s in ins] + [pl.BlockSpec(memory_space=pl.ANY)] * (len(held) + len(deps))
    lead = 0 if at is None else 1
    first_out = lead + len(arrays)

    def body(*refs):
        kernel(*refs[: lead + len(ins)], *refs[first_out:])

    moved = sum(x.size * x.dtype.itemsize for x, _ in ins)
    return pl.pallas_call(
        body,
        grid_spec=pltpu.PrefetchScalarGridSpec(
            num_scalar_prefetch=lead,
            grid=grid,
            in_specs=specs,
            out_specs=[o[2] for o in outs],
            scratch_shapes=scratch,
        ),
        out_shape=[jax.ShapeDtypeStruct(o[0], o[1]) for o in outs],
        input_output_aliases={lead + len(ins) + k: n for k, (n, _) in enumerate(held)},
        compiler_params=pltpu.CompilerParams(vmem_limit_bytes=VMEM_LIMIT),
        cost_estimate=pl.CostEstimate(flops=flops, bytes_accessed=moved, transcendentals=exps),
        name=name,
    )(*([] if at is None else [at]), *arrays)


def hidden_kernel(gate_ref, up_ref, out_ref):
    gate = gate_ref[...].astype(F32)
    hidden = gate * jax.nn.sigmoid(gate) * up_ref[...].astype(F32)
    out_ref[...] = jnp.transpose(hidden).astype(BF16)


def hidden_transposed(gate, up):
    tokens, width = gate.shape
    step = divisor(width, 1664, 128)
    spec = pl.BlockSpec((tokens, step), lambda i: (0, i))
    out = ((width, tokens), BF16, pl.BlockSpec((step, tokens), lambda i: (i, 0)), None)
    return run(hidden_kernel, "hidden", (width // step,), [(gate, spec), (up, spec)], [out])[0]


def product_kernel(choices, counts, ordering, at_ref, weight_ref, *refs):
    sources, outs = refs[:choices], refs[choices:-3]
    dy_ref, sems, out_sem = refs[-3:]
    step = pl.program_id(0)
    block = dy_ref.shape[0] // 2
    to_order = None
    if ordering:
        place = outs[-1].at[pl.ds(pl.multiple_of(at_ref[3] * 2 * block, 2 * block), 2 * block)]
        to_order = pltpu.make_async_copy(dy_ref, place, out_sem)

    @pl.when(step == 0)
    def _():
        for n, source in enumerate(sources):

            @pl.when(at_ref[4] == n)
            def _():
                copies = []
                for side in range(2):
                    rows = pl.ds(pl.multiple_of(at_ref[1 + side] * block, block), block)
                    copies.append(
                        pltpu.make_async_copy(
                            source.at[rows], dy_ref.at[pl.ds(side * block, block)], sems.at[side]
                        )
                    )
                for copy in copies:
                    copy.start()
                for copy in copies:
                    copy.wait()

        if ordering:
            to_order.start()

    part = lax.dot_general(
        weight_ref[...], dy_ref[...], (((1,), (1,)), ((), ())), preferred_element_type=F32
    )
    first = 0
    for q, count in enumerate(counts):

        @pl.when((step >= first) & (step < first + count))
        def _():
            outs[2 * q][...] = part[:, :block][None]
            outs[2 * q + 1][...] = part[:, block:].astype(BF16)[None]

        first += count

    if ordering:

        @pl.when(step == pl.num_programs(0) - 1)
        def _():
            to_order.wait()


def hidden_grad_terms(at, sources, weight, first, widths, held, ordered, total, deps):
    block, depth = sources[0].shape[0] // 2, sources[0].shape[1]
    tall = divisor(math.gcd(first, *widths), 832, 16)
    counts = [w // tall for w in widths]
    ins = [(weight, pl.BlockSpec((tall, depth), lambda i, at: (first // tall + i, 0)))]
    ins += [(x, pl.BlockSpec(memory_space=pl.ANY)) for x in sources]
    outs, start = [], 0
    for q, (w, count) in enumerate(zip(widths, counts)):

        def place(i, at, where=0 if q % 2 == 0 else 5, start=start, count=count):
            return (at[where], jnp.clip(i - start, 0, count - 1), 0)

        spec = pl.BlockSpec((1, tall, block), place)
        shape = (total // (2 * block), w, block)
        outs += [(shape, F32, spec, held[q][0]), (shape, BF16, spec, held[q][1])]
        start += count
    if ordered is not None:
        outs.append(((total, depth), BF16, pl.BlockSpec(memory_space=pl.ANY), ordered[0]))
    kernel = functools.partial(product_kernel, len(sources), counts, ordered is not None)
    scratch = [
        pltpu.VMEM((2 * block, depth), BF16),
        pltpu.SemaphoreType.DMA((2,)),
        pltpu.SemaphoreType.DMA,
    ]
    flops = 4 * block * depth * sum(widths)
    return run(kernel, "hidden_grad_terms", (start,), ins, outs, deps, at, scratch, flops)


def stage_kernel(*refs):
    refs[-1][...] = sum(ref[...].astype(F32) for ref in refs[:-1]).astype(BF16)


def stage_sum(terms, rows, deps):
    width, block = terms[0].shape[1:]
    tall = divisor(width, 416, 16)
    ins = [(t, pl.BlockSpec((rows, tall, block), lambda i: (1, i, 0))) for t in terms]
    out = ((rows, width, block), BF16, pl.BlockSpec((rows, tall, block), lambda i: (0, i, 0)), None)
    return run(stage_kernel, "stage_sum", (width // tall,), ins, [out], deps)[0]


def finish_kernel(gate_ref, up_ref, *refs):
    grad_hidden = jnp.transpose(sum(ref[0].astype(F32) for ref in refs[:-2]))
    gate, up = gate_ref[...].astype(F32), up_ref[...].astype(F32)
    sig = jax.nn.sigmoid(gate)
    refs[-2][...] = (grad_hidden * up * sig * (1.0 + gate * (1.0 - sig))).astype(BF16)
    refs[-1][...] = (grad_hidden * (gate * sig)).astype(BF16)


def finish(gate, up, terms, first, width, held, deps):
    tokens = gate.shape[0]
    window = pl.BlockSpec((pl.Element(tokens), pl.Element(width)), lambda i: (0, first))
    ins = [(gate, window), (up, window)]
    ins += [(t, pl.BlockSpec((1, width, tokens), lambda i: (0, 0, 0))) for t in terms]
    outs = [(gate.shape, BF16, window, x) for x in held]
    return run(finish_kernel, "finish", (1,), ins, outs, deps, exps=tokens * width)


def weight_grad_kernel(*refs):
    hidden = jnp.concatenate([ref[...] for ref in refs[:-2]], axis=1)
    refs[-1][...] = jnp.dot(hidden, refs[-2][...], preferred_element_type=F32).astype(BF16)


def weight_grad(pieces, dy, whole, total, start, rows, deps):
    block = pieces[0][0].shape[1]
    tokens, depth = dy.shape
    wide = divisor(depth, 256, 128)

    def spec(base):
        return pl.BlockSpec((rows, block), lambda i: ((start - base) // rows, 0))

    ins = [(x, spec(base)) for x, base in pieces]
    ins.append((dy, pl.BlockSpec((tokens, wide), lambda i: (0, i))))
    out = ((total, depth), BF16, pl.BlockSpec((rows, wide), lambda i: (start // rows, i)), whole)
    flops = 2 * rows * tokens * depth
    return run(weight_grad_kernel, "weight_grad", (depth // wide,), ins, [out], deps, flops=flops)[0]


def arrivals(z, count):
    found = []
    for s in range(1, count):
        if z - s >= 0:
            found.append(("up", s, z - s))
        if z + s < count:
            found.append(("down", s, z + s))
    return found


def pick(table, index):
    value = jnp.int32(table[0])
    for n in range(1, len(table)):
        value = jnp.where(index == n, jnp.int32(table[n]), value)
    return value


def program(row_count, col_count, grad_out, gate_act, up_act, down_weight):
    assert row_count == 2 * col_count
    row = lax.axis_index("row").astype(jnp.int32)
    col = lax.axis_index("col").astype(jnp.int32)
    core, chip = row % 2, row // 2
    bits = []
    while 2 ** (len(bits) + 1) < row_count:
        bits.append(2 ** (len(bits) + 1))
    streams = (bits, bits[::-1])
    width = down_weight.shape[0]
    block = gate_act.shape[0]
    tokens = row_count * block

    def swap(x, bit):
        pairs = [(r, r ^ bit) for r in range(row_count)]
        return jax.tree.map(lambda x: lax.ppermute(x, "row", pairs), x)

    places = []
    for order in streams:
        found = [0]
        for bit in order[::-1]:
            found = found + [f | bit // 2 for f in found]
        places.append([found.index(m) for m in range(row_count // 2)])

    ways = {"up": [grad_out], "down": [grad_out]}

    def forward(s):
        up, down = ways["up"], ways["down"]
        up.append(lax.ppermute(up[-1], "col", [(i, i + 1) for i in range(s - 1, col_count - 1)]))
        down.append(lax.ppermute(down[-1], "col", [(i, i - 1) for i in range(1, col_count - s + 1)]))

    def arrived(k):
        sources = [arrivals(z, col_count)[k - 1] for z in range(col_count)]
        kinds = sorted(set((way, s) for way, s, _ in sources))
        which = pick([kinds.index((way, s)) for way, s, _ in sources], col)
        return [ways[way][s] for way, s in kinds], which, pick([c for _, _, c in sources], col)

    units = width // LANES
    edges = [units * q // CHUNKS * LANES for q in range(CHUNKS + 1)]
    widths = [b - a for a, b in zip(edges, edges[1:])]
    terms = [(None, None)] * CHUNKS
    ordered = None

    def product(chunks, dy, deps):
        nonlocal ordered
        sources, which, place = dy
        flip = chip ^ place
        at = jnp.stack([pick(places[0], flip), core, 1 - core, flip, which, pick(places[1], flip)])
        first, last = chunks[0], chunks[-1] + 1
        out = hidden_grad_terms(
            at,
            sources,
            down_weight,
            edges[first],
            widths[first:last],
            terms[first:last],
            (ordered,) if first == 0 else None,
            tokens,
            deps,
        )
        for n, q in enumerate(chunks):
            terms[q] = (out[2 * n], out[2 * n + 1])
        if first == 0:
            ordered = out[-1]
        return out[0]

    forward(1)
    hidden = hidden_transposed(gate_act, up_act)
    held, base = {0: [hidden]}, {0: [0]}
    first_bits = bits[:2]
    for bit in first_bits + [1]:
        held[bit], base[bit] = swap([hidden], bit), [0]
    half = width // 2

    last = hidden
    dy = [grad_out], jnp.int32(0), col
    both = []
    for k in range(1, col_count):
        last = product(range(CHUNKS), dy, [last] + (held[1] if k == 2 else []))
        if k == 2 and len(first_bits) == 2:
            a, b = first_bits
            held[a], held[b], last = lax.optimization_barrier((held[a], held[b], last))
            both = [jnp.concatenate(held[a] + held[b])]
        ways["up"][k], ways["down"][k], last, both = lax.optimization_barrier(
            (ways["up"][k], ways["down"][k], last, both)
        )
        terms[0] = (last, terms[0][1])
        if k + 1 < col_count:
            forward(k + 1)
        dy = arrived(k)
        if k == 2 and len(first_bits) == 2:
            held[a | b] = [swap(held[a][0][:half], b), swap(held[b][0][half:], a)]
            base[a | b] = [0, half]
            held[a | 1] = held[b | 1] = swap(both, 1)
            base[a | 1], base[b | 1] = [0], [-width]

    held, last = lax.optimization_barrier((held, last))
    terms[0] = (last, terms[0][1])
    for bit in bits[2:]:
        for f in [f for f in held if f | bit not in held]:
            held[f | bit], base[f | bit] = swap(held[f], bit), base[f]
    ready = jax.tree.leaves(held)
    for f in [f for f in held if f | 1 not in held]:
        held[f | 1], base[f | 1] = swap(held[f], 1), base[f]

    grad_gate = grad_up = grad_down = None
    sums, stages = [None] * CHUNKS, [0] * CHUNKS
    part = width // PARTS

    def step(kind, n, last):
        nonlocal grad_gate, grad_up, grad_down
        if kind == "P":
            chunks = range(CHUNKS * n // GROUPS, CHUNKS * (n + 1) // GROUPS)
            deps = ready if n == 0 else jax.tree.leaves(held) if n == 1 else []
            last = product(chunks, dy, [last] + deps)
            for q in chunks:
                sums[q] = [terms[q][0], swap(terms[q][1], 1)]
            return last
        if kind == "S":
            bit = streams[n % 2][stages[n]]
            stages[n] += 1
            send = stage_sum(sums[n], (row_count // 2) >> stages[n], [last])
            sums[n] = sums[n] + [swap(send, bit)]
            return send
        if kind == "F":
            grad_gate, grad_up = finish(
                gate_act, up_act, sums[n], edges[n], widths[n], (grad_gate, grad_up), [last]
            )
            return grad_up
        pieces = []
        for f in range(row_count):
            side = -1 if n * part >= half else 0
            pieces.append((held[f][side], base[f][side]))
        grad_down = weight_grad(pieces, ordered, grad_down, width, n * part, part, [last])
        return grad_down

    for item in " ".join(PLAN).split():
        kind, n = item[0], int(item[1:])
        while kind == "F" and stages[n] < len(bits):
            last = step("S", n, last)
        last = step(kind, n, last)
    return grad_gate, grad_up, grad_down


def solution(mesh):
    def local(*args):
        return program(mesh.shape["row"], mesh.shape["col"], *args)

    return jax.shard_map(
        local,
        mesh=mesh,
        in_specs=(P("col", "row"), P("row", "col"), P("row", "col"), P("col", "row")),
        out_specs=(P("row", "col"), P("row", "col"), P("col", "row")),
        check_vma=False,
    )
```

```python
import functools
import math

import jax
import jax.numpy as jnp
from jax import lax
from jax.experimental import pallas as pl
from jax.experimental.pallas import tpu as pltpu
from jax.sharding import PartitionSpec as P

F32, BF16 = jnp.float32, jnp.bfloat16
VMEM_LIMIT = 63 * 1024 * 1024
CHUNKS = 4
GROUPS = 2
PARTS = 4
LANES = 128
PLAN = ["P0 P1 S0 S1", "S2 S3 W0 S0", "S1 W1 W2 S2", "S3 W3 F0 F1", "F2 F3"]


def divisor(extent, most, step):
    best = extent
    for size in range(step, most + 1, step):
        if extent % size == 0:
            best = size
    return best


def run(kernel, name, grid, ins, outs, deps=(), at=None, scratch=(), flops=0, exps=0):
    held = [(n, o[3]) for n, o in enumerate(outs) if o[3] is not None]
    deps = [d for d in deps if not any(d is x for _, x in held)]
    arrays = [x for x, _ in ins] + [x for _, x in held] + list(deps)
    specs = [s for _, s in ins] + [pl.BlockSpec(memory_space=pl.ANY)] * (len(held) + len(deps))
    lead = 0 if at is None else 1
    first_out = lead + len(arrays)

    def body(*refs):
        kernel(*refs[: lead + len(ins)], *refs[first_out:])

    moved = sum(x.size * x.dtype.itemsize for x, _ in ins)
    return pl.pallas_call(
        body,
        grid_spec=pltpu.PrefetchScalarGridSpec(
            num_scalar_prefetch=lead,
            grid=grid,
            in_specs=specs,
            out_specs=[o[2] for o in outs],
            scratch_shapes=scratch,
        ),
        out_shape=[jax.ShapeDtypeStruct(o[0], o[1]) for o in outs],
        input_output_aliases={lead + len(ins) + k: n for k, (n, _) in enumerate(held)},
        compiler_params=pltpu.CompilerParams(vmem_limit_bytes=VMEM_LIMIT),
        cost_estimate=pl.CostEstimate(
            flops=flops, bytes_accessed=moved, transcendentals=exps
        ),
        name=name,
    )(*([] if at is None else [at]), *arrays)


def hidden_kernel(gate_ref, up_ref, out_ref):
    gate = gate_ref[...].astype(F32)
    hidden = gate * jax.nn.sigmoid(gate) * up_ref[...].astype(F32)
    out_ref[...] = jnp.transpose(hidden.astype(BF16))


def hidden_transposed(gate, up):
    tokens, width = gate.shape
    step = divisor(width, 1664, 128)
    spec = pl.BlockSpec((tokens, step), lambda i: (0, i))
    out = ((width, tokens), BF16, pl.BlockSpec((step, tokens), lambda i: (i, 0)), None)
    return run(hidden_kernel, "hidden", (width // step,), [(gate, spec), (up, spec)], [out])[0]


def product_kernel(choices, counts, ordering, at_ref, weight_ref, *refs):
    sources, outs = refs[:choices], refs[choices:-3]
    dy_ref, sems, out_sem = refs[-3:]
    step = pl.program_id(0)
    block = dy_ref.shape[0] // 2
    to_order = None
    if ordering:
        place = outs[-1].at[pl.ds(pl.multiple_of(at_ref[3] * 2 * block, 2 * block), 2 * block)]
        to_order = pltpu.make_async_copy(dy_ref, place, out_sem)

    @pl.when(step == 0)
    def _():
        for n, source in enumerate(sources):

            @pl.when(at_ref[4] == n)
            def _():
                copies = []
                for side in range(2):
                    rows = pl.ds(pl.multiple_of(at_ref[1 + side] * block, block), block)
                    copies.append(
                        pltpu.make_async_copy(
                            source.at[rows], dy_ref.at[pl.ds(side * block, block)], sems.at[side]
                        )
                    )
                for copy in copies:
                    copy.start()
                for copy in copies:
                    copy.wait()

        if ordering:
            to_order.start()

    half = weight_ref.shape[0] // 2
    parts = [
        lax.dot_general(
            weight_ref[pl.ds(n * half, half)],
            dy_ref[...],
            (((1,), (1,)), ((), ())),
            preferred_element_type=F32,
        )
        for n in range(2)
    ]
    first = 0
    for q, count in enumerate(counts):

        @pl.when((step >= first) & (step < first + count))
        def _():
            for n, part in enumerate(parts):
                outs[2 * q][0, pl.ds(n * half, half)] = part[:, :block]
                outs[2 * q + 1][0, pl.ds(n * half, half)] = part[:, block:].astype(BF16)

        first += count

    if ordering:

        @pl.when(step == pl.num_programs(0) - 1)
        def _():
            to_order.wait()


def hidden_grad_terms(at, sources, weight, first, widths, held, ordered, total, deps):
    block, depth = sources[0].shape[0] // 2, sources[0].shape[1]
    tall = divisor(math.gcd(first, *widths), 832, 32)
    counts = [w // tall for w in widths]
    ins = [(weight, pl.BlockSpec((tall, depth), lambda i, at: (first // tall + i, 0)))]
    ins += [(x, pl.BlockSpec(memory_space=pl.ANY)) for x in sources]
    outs, start = [], 0
    for q, (w, count) in enumerate(zip(widths, counts)):

        def place(i, at, where=0 if q % 2 == 0 else 5, start=start, count=count):
            return (at[where], jnp.clip(i - start, 0, count - 1), 0)

        spec = pl.BlockSpec((1, tall, block), place)
        shape = (total // (2 * block), w, block)
        outs += [(shape, F32, spec, held[q][0]), (shape, BF16, spec, held[q][1])]
        start += count
    if ordered is not None:
        outs.append(((total, depth), BF16, pl.BlockSpec(memory_space=pl.ANY), ordered[0]))
    kernel = functools.partial(product_kernel, len(sources), counts, ordered is not None)
    scratch = [
        pltpu.VMEM((2 * block, depth), BF16),
        pltpu.SemaphoreType.DMA((2,)),
        pltpu.SemaphoreType.DMA,
    ]
    flops = 4 * block * depth * sum(widths)
    return run(
        kernel, "hidden_grad_terms", (start,), ins, outs, deps, at, scratch, flops
    )


def finish_kernel(gate_ref, up_ref, *refs):
    grad_hidden = jnp.transpose(sum(ref[0].astype(F32) for ref in refs[:-2]))
    gate, up = gate_ref[...].astype(F32), up_ref[...].astype(F32)
    sig = jax.nn.sigmoid(gate)
    refs[-2][...] = (grad_hidden * up * sig * (1.0 + gate * (1.0 - sig))).astype(BF16)
    refs[-1][...] = (grad_hidden * (gate * sig)).astype(BF16)


def finish(gate, up, terms, first, width, held, deps):
    tokens = gate.shape[0]
    window = pl.BlockSpec((pl.Element(tokens), pl.Element(width)), lambda i: (0, first))
    ins = [(gate, window), (up, window)]
    ins += [(t, pl.BlockSpec((1, width, tokens), lambda i: (0, 0, 0))) for t in terms]
    outs = [(gate.shape, BF16, window, x) for x in held]
    return run(finish_kernel, "finish", (1,), ins, outs, deps, exps=tokens * width)


def weight_grad_kernel(*refs):
    hidden = jnp.concatenate([ref[...] for ref in refs[:-2]], axis=1)
    refs[-1][...] = jnp.dot(hidden, refs[-2][...], preferred_element_type=F32).astype(BF16)


def weight_grad(pieces, dy, whole, total, start, rows, deps):
    block = pieces[0][0].shape[1]
    tokens, depth = dy.shape
    tall, wide = divisor(rows, 832, 16), divisor(depth, 512, 128)

    def spec(base):
        return pl.BlockSpec((tall, block), lambda i, j: ((start - base) // tall + i, 0))

    ins = [(x, spec(base)) for x, base in pieces]
    ins.append((dy, pl.BlockSpec((tokens, wide), lambda i, j: (0, j))))
    place = pl.BlockSpec((tall, wide), lambda i, j: (start // tall + i, j))
    out = ((total, depth), BF16, place, whole)
    grid = (rows // tall, depth // wide)
    flops = 2 * rows * tokens * depth
    return run(weight_grad_kernel, "weight_grad", grid, ins, [out], deps, flops=flops)[0]


def arrivals(z, count):
    found = []
    for s in range(1, count):
        if z - s >= 0:
            found.append(("up", s, z - s))
        if z + s < count:
            found.append(("down", s, z + s))
    return found


def pick(table, index):
    value = jnp.int32(table[0])
    for n in range(1, len(table)):
        value = jnp.where(index == n, jnp.int32(table[n]), value)
    return value


def program(row_count, col_count, grad_out, gate_act, up_act, down_weight):
    assert row_count == 2 * col_count
    row = lax.axis_index("row").astype(jnp.int32)
    col = lax.axis_index("col").astype(jnp.int32)
    core, chip = row % 2, row // 2
    bits = []
    while 2 ** (len(bits) + 1) < row_count:
        bits.append(2 ** (len(bits) + 1))
    streams = (bits, bits[::-1])
    width = down_weight.shape[0]
    block = gate_act.shape[0]
    tokens = row_count * block

    def swap(x, bit):
        pairs = [(r, r ^ bit) for r in range(row_count)]
        return jax.tree.map(lambda x: lax.ppermute(x, "row", pairs), x)

    places = []
    for order in streams:
        found = [0]
        for bit in order[::-1]:
            found = found + [f | bit // 2 for f in found]
        places.append([found.index(m) for m in range(row_count // 2)])

    ways = {"up": [grad_out], "down": [grad_out]}

    def forward(s):
        up, down = ways["up"], ways["down"]
        up.append(lax.ppermute(up[-1], "col", [(i, i + 1) for i in range(s - 1, col_count - 1)]))
        down.append(lax.ppermute(down[-1], "col", [(i, i - 1) for i in range(1, col_count - s + 1)]))

    def arrived(k):
        sources = [arrivals(z, col_count)[k - 1] for z in range(col_count)]
        kinds = sorted(set((way, s) for way, s, _ in sources))
        which = pick([kinds.index((way, s)) for way, s, _ in sources], col)
        return [ways[way][s] for way, s in kinds], which, pick([c for _, _, c in sources], col)

    units = width // LANES
    edges = [units * q // CHUNKS * LANES for q in range(CHUNKS + 1)]
    widths = [b - a for a, b in zip(edges, edges[1:])]
    terms = [(None, None)] * CHUNKS
    ordered = None

    def product(chunks, dy, deps):
        nonlocal ordered
        sources, which, place = dy
        flip = chip ^ place
        at = jnp.stack([pick(places[0], flip), core, 1 - core, flip, which, pick(places[1], flip)])
        first, last = chunks[0], chunks[-1] + 1
        out = hidden_grad_terms(
            at,
            sources,
            down_weight,
            edges[first],
            widths[first:last],
            terms[first:last],
            (ordered,) if first == 0 else None,
            tokens,
            deps,
        )
        for n, q in enumerate(chunks):
            terms[q] = (out[2 * n], out[2 * n + 1])
        if first == 0:
            ordered = out[-1]
        return out[0]

    forward(1)
    hidden = hidden_transposed(gate_act, up_act)
    held, base = {0: [hidden]}, {0: [0]}
    first_bits = bits[:2]
    for bit in first_bits + [1]:
        held[bit], base[bit] = swap([hidden], bit), [0]
    half = width // 2

    last = hidden
    dy = [grad_out], jnp.int32(0), col
    both = []
    for k in range(1, col_count):
        last = product(range(CHUNKS), dy, [last] + (held[1] if k == 2 else []))
        if k == 2 and len(first_bits) == 2:
            a, b = first_bits
            held[a], held[b], last = lax.optimization_barrier((held[a], held[b], last))
            both = [jnp.concatenate(held[a] + held[b])]
        ways["up"][k], ways["down"][k], last, both = lax.optimization_barrier(
            (ways["up"][k], ways["down"][k], last, both)
        )
        terms[0] = (last, terms[0][1])
        if k + 1 < col_count:
            forward(k + 1)
        dy = arrived(k)
        if k == 2 and len(first_bits) == 2:
            held[a | b] = [swap(held[a][0][:half], b), swap(held[b][0][half:], a)]
            base[a | b] = [0, half]
            held[a | 1] = held[b | 1] = swap(both, 1)
            base[a | 1], base[b | 1] = [0], [-width]

    held, last = lax.optimization_barrier((held, last))
    terms[0] = (last, terms[0][1])
    for bit in bits[2:]:
        for f in [f for f in held if f | bit not in held]:
            held[f | bit], base[f | bit] = swap(held[f], bit), base[f]
    ready = jax.tree.leaves(held)
    for f in [f for f in held if f | 1 not in held]:
        held[f | 1], base[f | 1] = swap(held[f], 1), base[f]

    grad_gate = grad_up = grad_down = None
    sums, stages = [None] * CHUNKS, [0] * CHUNKS
    part = width // PARTS

    def step(kind, n, last):
        nonlocal grad_gate, grad_up, grad_down
        if kind == "P":
            chunks = range(CHUNKS * n // GROUPS, CHUNKS * (n + 1) // GROUPS)
            deps = ready if n == 0 else jax.tree.leaves(held) if n == 1 else []
            last = product(chunks, dy, [last] + deps)
            for q in chunks:
                sums[q] = [terms[q][0], swap(terms[q][1], 1)]
            return last
        if kind == "S":
            bit = streams[n % 2][stages[n]]
            stages[n] += 1
            rows = (row_count // 2) >> stages[n]
            is_whole = last is grad_down
            sums[n], last = lax.optimization_barrier((sums[n], last))
            if is_whole:
                grad_down = last
            send = sum(t[rows : 2 * rows].astype(F32) for t in sums[n]).astype(BF16)
            sums[n] = sums[n] + [swap(send, bit)]
            return send
        if kind == "F":
            grad_gate, grad_up = finish(
                gate_act, up_act, sums[n], edges[n], widths[n], (grad_gate, grad_up), [last]
            )
            return grad_up
        pieces = []
        for f in range(row_count):
            side = -1 if n * part >= half else 0
            pieces.append((held[f][side], base[f][side]))
        grad_down = weight_grad(pieces, ordered, grad_down, width, n * part, part, [last])
        return grad_down

    for item in " ".join(PLAN).split():
        kind, n = item[0], int(item[1:])
        while kind == "F" and stages[n] < len(bits):
            last = step("S", n, last)
        last = step(kind, n, last)
    return grad_gate, grad_up, grad_down


def solution(mesh):
    def local(*args):
        return program(mesh.shape["row"], mesh.shape["col"], *args)

    return jax.shard_map(
        local,
        mesh=mesh,
        in_specs=(P("col", "row"), P("row", "col"), P("row", "col"), P("col", "row")),
        out_specs=(P("row", "col"), P("row", "col"), P("col", "row")),
        check_vma=False,
    )
```

```python
import functools
import math

import jax
import jax.numpy as jnp
from jax import lax
from jax.experimental import pallas as pl
from jax.experimental.pallas import tpu as pltpu
from jax.sharding import PartitionSpec as P

F32, BF16 = jnp.float32, jnp.bfloat16
VMEM_LIMIT = 63 * 1024 * 1024
CHUNKS = 4
GROUPS = 2
PARTS = 4
LANES = 128
PLAN = ["P0 P1 S0 S1", "S2 S3 W0 S0", "S1 W1 W2 S2", "S3 W3 F0 F1", "F2 F3"]


def divisor(extent, most, step):
    best = extent
    for size in range(step, most + 1, step):
        if extent % size == 0:
            best = size
    return best


def run(kernel, name, grid, ins, outs, deps=(), at=None, scratch=(), flops=0, exps=0):
    held = [(n, o[3]) for n, o in enumerate(outs) if o[3] is not None]
    deps = [d for d in deps if not any(d is x for _, x in held)]
    arrays = [x for x, _ in ins] + [x for _, x in held] + list(deps)
    specs = [s for _, s in ins] + [pl.BlockSpec(memory_space=pl.ANY)] * (len(held) + len(deps))
    lead = 0 if at is None else 1
    first_out = lead + len(arrays)

    def body(*refs):
        kernel(*refs[: lead + len(ins)], *refs[first_out:])

    moved = sum(x.size * x.dtype.itemsize for x, _ in ins)
    return pl.pallas_call(
        body,
        grid_spec=pltpu.PrefetchScalarGridSpec(
            num_scalar_prefetch=lead,
            grid=grid,
            in_specs=specs,
            out_specs=[o[2] for o in outs],
            scratch_shapes=scratch,
        ),
        out_shape=[jax.ShapeDtypeStruct(o[0], o[1]) for o in outs],
        input_output_aliases={lead + len(ins) + k: n for k, (n, _) in enumerate(held)},
        compiler_params=pltpu.CompilerParams(vmem_limit_bytes=VMEM_LIMIT),
        cost_estimate=pl.CostEstimate(
            flops=flops, bytes_accessed=moved, transcendentals=exps
        ),
        name=name,
    )(*([] if at is None else [at]), *arrays)


def hidden_kernel(gate_ref, up_ref, out_ref):
    gate = gate_ref[...].astype(F32)
    hidden = gate * jax.nn.sigmoid(gate) * up_ref[...].astype(F32)
    out_ref[...] = jnp.transpose(hidden.astype(BF16))


def hidden_transposed(gate, up):
    tokens, width = gate.shape
    step = divisor(width, 1664, 128)
    spec = pl.BlockSpec((tokens, step), lambda i: (0, i))
    out = ((width, tokens), BF16, pl.BlockSpec((step, tokens), lambda i: (i, 0)), None)
    return run(hidden_kernel, "hidden", (width // step,), [(gate, spec), (up, spec)], [out])[0]


def product_kernel(choices, counts, ordering, at_ref, weight_ref, *refs):
    sources, outs = refs[:choices], refs[choices:-4]
    dy_ref, turned_ref, sems, out_sem = refs[-4:]
    step = pl.program_id(0)
    block = dy_ref.shape[0] // 2
    to_order = None
    if ordering:
        place = outs[-1].at[pl.ds(pl.multiple_of(at_ref[3] * 2 * block, 2 * block), 2 * block)]
        to_order = pltpu.make_async_copy(dy_ref, place, out_sem)

    @pl.when(step == 0)
    def _():
        for n, source in enumerate(sources):

            @pl.when(at_ref[4] == n)
            def _():
                copies = []
                for side in range(2):
                    rows = pl.ds(pl.multiple_of(at_ref[1 + side] * block, block), block)
                    copies.append(
                        pltpu.make_async_copy(
                            source.at[rows], dy_ref.at[pl.ds(side * block, block)], sems.at[side]
                        )
                    )
                for copy in copies:
                    copy.start()
                for copy in copies:
                    copy.wait()

        if ordering:
            to_order.start()
        turned_ref[...] = jnp.transpose(dy_ref[...])

    part = jnp.dot(weight_ref[...], turned_ref[...], preferred_element_type=F32)
    first = 0
    for q, count in enumerate(counts):

        @pl.when((step >= first) & (step < first + count))
        def _():
            outs[2 * q][...] = part[:, :block][None]
            outs[2 * q + 1][...] = part[:, block:].astype(BF16)[None]

        first += count

    if ordering:

        @pl.when(step == pl.num_programs(0) - 1)
        def _():
            to_order.wait()


def hidden_grad_terms(at, sources, weight, first, widths, held, ordered, total, deps):
    block, depth = sources[0].shape[0] // 2, sources[0].shape[1]
    tall = divisor(math.gcd(first, *widths), 832, 16)
    counts = [w // tall for w in widths]
    ins = [(weight, pl.BlockSpec((tall, depth), lambda i, at: (first // tall + i, 0)))]
    ins += [(x, pl.BlockSpec(memory_space=pl.ANY)) for x in sources]
    outs, start = [], 0
    for q, (w, count) in enumerate(zip(widths, counts)):

        def place(i, at, where=0 if q % 2 == 0 else 5, start=start, count=count):
            return (at[where], jnp.clip(i - start, 0, count - 1), 0)

        spec = pl.BlockSpec((1, tall, block), place)
        shape = (total // (2 * block), w, block)
        outs += [(shape, F32, spec, held[q][0]), (shape, BF16, spec, held[q][1])]
        start += count
    if ordered is not None:
        outs.append(((total, depth), BF16, pl.BlockSpec(memory_space=pl.ANY), ordered[0]))
    kernel = functools.partial(product_kernel, len(sources), counts, ordered is not None)
    scratch = [
        pltpu.VMEM((2 * block, depth), BF16),
        pltpu.VMEM((depth, 2 * block), BF16),
        pltpu.SemaphoreType.DMA((2,)),
        pltpu.SemaphoreType.DMA,
    ]
    flops = 4 * block * depth * sum(widths)
    return run(
        kernel, "hidden_grad_terms", (start,), ins, outs, deps, at, scratch, flops
    )


def finish_kernel(gate_ref, up_ref, *refs):
    grad_hidden = jnp.transpose(sum(ref[0].astype(F32) for ref in refs[:-2]))
    gate, up = gate_ref[...].astype(F32), up_ref[...].astype(F32)
    sig = jax.nn.sigmoid(gate)
    refs[-2][...] = (grad_hidden * up * sig * (1.0 + gate * (1.0 - sig))).astype(BF16)
    refs[-1][...] = (grad_hidden * (gate * sig)).astype(BF16)


def finish(gate, up, terms, first, width, held, deps):
    tokens = gate.shape[0]
    window = pl.BlockSpec((pl.Element(tokens), pl.Element(width)), lambda i: (0, first))
    ins = [(gate, window), (up, window)]
    ins += [(t, pl.BlockSpec((1, width, tokens), lambda i: (0, 0, 0))) for t in terms]
    outs = [(gate.shape, BF16, window, x) for x in held]
    return run(finish_kernel, "finish", (1,), ins, outs, deps, exps=tokens * width)


def weight_grad_kernel(*refs):
    hidden = jnp.concatenate([ref[...] for ref in refs[:-2]], axis=1)
    refs[-1][...] = jnp.dot(hidden, refs[-2][...], preferred_element_type=F32).astype(BF16)


def weight_grad(pieces, dy, whole, total, start, rows, deps):
    block = pieces[0][0].shape[1]
    tokens, depth = dy.shape
    tall, wide = divisor(rows, 832, 16), divisor(depth, 1024, 128)

    def spec(base):
        return pl.BlockSpec((tall, block), lambda i, j: ((start - base) // tall + i, 0))

    ins = [(x, spec(base)) for x, base in pieces]
    ins.append((dy, pl.BlockSpec((tokens, wide), lambda i, j: (0, j))))
    place = pl.BlockSpec((tall, wide), lambda i, j: (start // tall + i, j))
    out = ((total, depth), BF16, place, whole)
    grid = (rows // tall, depth // wide)
    flops = 2 * rows * tokens * depth
    return run(weight_grad_kernel, "weight_grad", grid, ins, [out], deps, flops=flops)[0]


def arrivals(z, count):
    found = []
    for s in range(1, count):
        if z - s >= 0:
            found.append(("up", s, z - s))
        if z + s < count:
            found.append(("down", s, z + s))
    return found


def pick(table, index):
    value = jnp.int32(table[0])
    for n in range(1, len(table)):
        value = jnp.where(index == n, jnp.int32(table[n]), value)
    return value


def program(row_count, col_count, grad_out, gate_act, up_act, down_weight):
    assert row_count == 2 * col_count
    row = lax.axis_index("row").astype(jnp.int32)
    col = lax.axis_index("col").astype(jnp.int32)
    core, chip = row % 2, row // 2
    bits = []
    while 2 ** (len(bits) + 1) < row_count:
        bits.append(2 ** (len(bits) + 1))
    streams = (bits, bits[::-1])
    width = down_weight.shape[0]
    block = gate_act.shape[0]
    tokens = row_count * block

    def swap(x, bit):
        pairs = [(r, r ^ bit) for r in range(row_count)]
        return jax.tree.map(lambda x: lax.ppermute(x, "row", pairs), x)

    places = []
    for order in streams:
        found = [0]
        for bit in order[::-1]:
            found = found + [f | bit // 2 for f in found]
        places.append([found.index(m) for m in range(row_count // 2)])

    ways = {"up": [grad_out], "down": [grad_out]}

    def forward(s):
        up, down = ways["up"], ways["down"]
        up.append(lax.ppermute(up[-1], "col", [(i, i + 1) for i in range(s - 1, col_count - 1)]))
        down.append(lax.ppermute(down[-1], "col", [(i, i - 1) for i in range(1, col_count - s + 1)]))

    def arrived(k):
        sources = [arrivals(z, col_count)[k - 1] for z in range(col_count)]
        kinds = sorted(set((way, s) for way, s, _ in sources))
        which = pick([kinds.index((way, s)) for way, s, _ in sources], col)
        return [ways[way][s] for way, s in kinds], which, pick([c for _, _, c in sources], col)

    units = width // LANES
    edges = [units * q // CHUNKS * LANES for q in range(CHUNKS + 1)]
    widths = [b - a for a, b in zip(edges, edges[1:])]
    terms = [(None, None)] * CHUNKS
    ordered = None

    def product(chunks, dy, deps):
        nonlocal ordered
        sources, which, place = dy
        flip = chip ^ place
        at = jnp.stack([pick(places[0], flip), core, 1 - core, flip, which, pick(places[1], flip)])
        first, last = chunks[0], chunks[-1] + 1
        out = hidden_grad_terms(
            at,
            sources,
            down_weight,
            edges[first],
            widths[first:last],
            terms[first:last],
            (ordered,) if first == 0 else None,
            tokens,
            deps,
        )
        for n, q in enumerate(chunks):
            terms[q] = (out[2 * n], out[2 * n + 1])
        if first == 0:
            ordered = out[-1]
        return out[0]

    forward(1)
    hidden = hidden_transposed(gate_act, up_act)
    held, base = {0: [hidden]}, {0: [0]}
    first_bits = bits[:2]
    for bit in first_bits + [1]:
        held[bit], base[bit] = swap([hidden], bit), [0]
    half = width // 2

    last = hidden
    dy = [grad_out], jnp.int32(0), col
    both = []
    for k in range(1, col_count):
        last = product(range(CHUNKS), dy, [last] + (held[1] if k == 2 else []))
        if k == 2 and len(first_bits) == 2:
            a, b = first_bits
            held[a], held[b], last = lax.optimization_barrier((held[a], held[b], last))
            both = [jnp.concatenate(held[a] + held[b])]
        ways["up"][k], ways["down"][k], last, both = lax.optimization_barrier(
            (ways["up"][k], ways["down"][k], last, both)
        )
        terms[0] = (last, terms[0][1])
        if k + 1 < col_count:
            forward(k + 1)
        dy = arrived(k)
        if k == 2 and len(first_bits) == 2:
            held[a | b] = [swap(held[a][0][:half], b), swap(held[b][0][half:], a)]
            base[a | b] = [0, half]
            held[a | 1] = held[b | 1] = swap(both, 1)
            base[a | 1], base[b | 1] = [0], [-width]

    held, last = lax.optimization_barrier((held, last))
    terms[0] = (last, terms[0][1])
    for bit in bits[2:]:
        for f in [f for f in held if f | bit not in held]:
            held[f | bit], base[f | bit] = swap(held[f], bit), base[f]
    ready = jax.tree.leaves(held)
    for f in [f for f in held if f | 1 not in held]:
        held[f | 1], base[f | 1] = swap(held[f], 1), base[f]

    grad_gate = grad_up = grad_down = None
    sums, stages = [None] * CHUNKS, [0] * CHUNKS
    part = width // PARTS

    def step(kind, n, last):
        nonlocal grad_gate, grad_up, grad_down
        if kind == "P":
            chunks = range(CHUNKS * n // GROUPS, CHUNKS * (n + 1) // GROUPS)
            deps = ready if n == 0 else jax.tree.leaves(held) if n == 1 else []
            last = product(chunks, dy, [last] + deps)
            for q in chunks:
                sums[q] = [terms[q][0], swap(terms[q][1], 1)]
            return last
        if kind == "S":
            bit = streams[n % 2][stages[n]]
            stages[n] += 1
            rows = (row_count // 2) >> stages[n]
            is_whole = last is grad_down
            sums[n], last = lax.optimization_barrier((sums[n], last))
            if is_whole:
                grad_down = last
            send = sum(t[rows : 2 * rows].astype(F32) for t in sums[n]).astype(BF16)
            sums[n] = sums[n] + [swap(send, bit)]
            return send
        if kind == "F":
            grad_gate, grad_up = finish(
                gate_act, up_act, sums[n], edges[n], widths[n], (grad_gate, grad_up), [last]
            )
            return grad_up
        pieces = []
        for f in range(row_count):
            side = -1 if n * part >= half else 0
            pieces.append((held[f][side], base[f][side]))
        grad_down = weight_grad(pieces, ordered, grad_down, width, n * part, part, [last])
        return grad_down

    for item in " ".join(PLAN).split():
        kind, n = item[0], int(item[1:])
        while kind == "F" and stages[n] < len(bits):
            last = step("S", n, last)
        last = step(kind, n, last)
    return grad_gate, grad_up, grad_down


def solution(mesh):
    def local(*args):
        return program(mesh.shape["row"], mesh.shape["col"], *args)

    return jax.shard_map(
        local,
        mesh=mesh,
        in_specs=(P("col", "row"), P("row", "col"), P("row", "col"), P("col", "row")),
        out_specs=(P("row", "col"), P("row", "col"), P("col", "row")),
        check_vma=False,
    )
```

```python
import functools
import math

import jax
import jax.numpy as jnp
from jax import lax
from jax.experimental import pallas as pl
from jax.experimental.pallas import tpu as pltpu
from jax.sharding import PartitionSpec as P

F32, BF16 = jnp.float32, jnp.bfloat16
VMEM_LIMIT = 63 * 1024 * 1024
CHUNKS = 4
GROUPS = 2
PARTS = [(0, 2), (2, 3), (3, 4)]
SPLIT = 4
LANES = 128
PLAN = ["P0 P1 S0 S1", "S2 S3 W0 S0", "S1 W1 S2 S3", "W2 F0 F1 F2", "F3"]


def divisor(extent, most, step):
    best = extent
    for size in range(step, most + 1, step):
        if extent % size == 0:
            best = size
    return best


def run(kernel, name, grid, ins, outs, deps=(), at=None, scratch=(), flops=0, exps=0):
    held = [(n, o[3]) for n, o in enumerate(outs) if o[3] is not None]
    deps = [d for d in deps if not any(d is x for _, x in held)]
    arrays = [x for x, _ in ins] + [x for _, x in held] + list(deps)
    specs = [s for _, s in ins] + [pl.BlockSpec(memory_space=pl.ANY)] * (len(held) + len(deps))
    lead = 0 if at is None else 1
    first_out = lead + len(arrays)

    def body(*refs):
        kernel(*refs[: lead + len(ins)], *refs[first_out:])

    moved = sum(x.size * x.dtype.itemsize for x, _ in ins)
    return pl.pallas_call(
        body,
        grid_spec=pltpu.PrefetchScalarGridSpec(
            num_scalar_prefetch=lead,
            grid=grid,
            in_specs=specs,
            out_specs=[o[2] for o in outs],
            scratch_shapes=scratch,
        ),
        out_shape=[jax.ShapeDtypeStruct(o[0], o[1]) for o in outs],
        input_output_aliases={lead + len(ins) + k: n for k, (n, _) in enumerate(held)},
        compiler_params=pltpu.CompilerParams(vmem_limit_bytes=VMEM_LIMIT),
        cost_estimate=pl.CostEstimate(
            flops=flops, bytes_accessed=moved, transcendentals=exps
        ),
        name=name,
    )(*([] if at is None else [at]), *arrays)


def hidden_kernel(gate_ref, up_ref, out_ref):
    gate = gate_ref[...].astype(F32)
    hidden = gate * jax.nn.sigmoid(gate) * up_ref[...].astype(F32)
    out_ref[...] = jnp.transpose(hidden.astype(BF16))


def hidden_transposed(gate, up):
    tokens, width = gate.shape
    step = divisor(width, 1664, 128)
    spec = pl.BlockSpec((tokens, step), lambda i: (0, i))
    out = ((width, tokens), BF16, pl.BlockSpec((step, tokens), lambda i: (i, 0)), None)
    return run(hidden_kernel, "hidden", (width // step,), [(gate, spec), (up, spec)], [out])[0]


def product_kernel(choices, counts, ordering, at_ref, *refs):
    weights, refs = refs[:SPLIT], refs[SPLIT:]
    sources, outs = refs[:choices], refs[choices:-4]
    dy_ref, turned_ref, sems, out_sem = refs[-4:]
    step = pl.program_id(0)
    block = dy_ref.shape[0] // 2
    to_order = None
    if ordering:
        place = outs[-1].at[pl.ds(pl.multiple_of(at_ref[3] * 2 * block, 2 * block), 2 * block)]
        to_order = pltpu.make_async_copy(dy_ref, place, out_sem)

    @pl.when(step == 0)
    def _():
        for n, source in enumerate(sources):

            @pl.when(at_ref[4] == n)
            def _():
                copies = []
                for side in range(2):
                    rows = pl.ds(pl.multiple_of(at_ref[1 + side] * block, block), block)
                    copies.append(
                        pltpu.make_async_copy(
                            source.at[rows], dy_ref.at[pl.ds(side * block, block)], sems.at[side]
                        )
                    )
                for copy in copies:
                    copy.start()
                for copy in copies:
                    copy.wait()

        if ordering:
            to_order.start()
        turned_ref[...] = jnp.transpose(dy_ref[...])

    turned = turned_ref[...]
    parts = [jnp.dot(ref[...], turned, preferred_element_type=F32) for ref in weights]
    rows = weights[0].shape[0]
    first = 0
    for q, count in enumerate(counts):

        @pl.when((step >= first) & (step < first + count))
        def _():
            for n, part in enumerate(parts):
                outs[2 * q][0, pl.ds(n * rows, rows)] = part[:, :block]
                outs[2 * q + 1][0, pl.ds(n * rows, rows)] = part[:, block:].astype(BF16)

        first += count

    if ordering:

        @pl.when(step == pl.num_programs(0) - 1)
        def _():
            to_order.wait()


def hidden_grad_terms(at, sources, weight, first, widths, held, ordered, total, deps):
    block, depth = sources[0].shape[0] // 2, sources[0].shape[1]
    tall = divisor(math.gcd(first, *widths), 832, 16 * SPLIT)
    counts = [w // tall for w in widths]

    def weight_spec(n):
        start = first // tall
        return pl.BlockSpec((tall // SPLIT, depth), lambda i, at: ((start + i) * SPLIT + n, 0))

    ins = [(weight, weight_spec(n)) for n in range(SPLIT)]
    ins += [(x, pl.BlockSpec(memory_space=pl.ANY)) for x in sources]
    outs, start = [], 0
    for q, (w, count) in enumerate(zip(widths, counts)):

        def place(i, at, where=0 if q % 2 == 0 else 5, start=start, count=count):
            return (at[where], jnp.clip(i - start, 0, count - 1), 0)

        spec = pl.BlockSpec((1, tall, block), place)
        shape = (total // (2 * block), w, block)
        outs += [(shape, F32, spec, held[q][0]), (shape, BF16, spec, held[q][1])]
        start += count
    if ordered is not None:
        outs.append(((total, depth), BF16, pl.BlockSpec(memory_space=pl.ANY), ordered[0]))
    kernel = functools.partial(product_kernel, len(sources), counts, ordered is not None)
    scratch = [
        pltpu.VMEM((2 * block, depth), BF16),
        pltpu.VMEM((depth, 2 * block), BF16),
        pltpu.SemaphoreType.DMA((2,)),
        pltpu.SemaphoreType.DMA,
    ]
    flops = 4 * block * depth * sum(widths)
    return run(
        kernel, "hidden_grad_terms", (start,), ins, outs, deps, at, scratch, flops
    )


def finish_kernel(gate_ref, up_ref, *refs):
    grad_hidden = jnp.transpose(sum(ref[0].astype(F32) for ref in refs[:-2]))
    gate, up = gate_ref[...].astype(F32), up_ref[...].astype(F32)
    sig = jax.nn.sigmoid(gate)
    refs[-2][...] = (grad_hidden * up * sig * (1.0 + gate * (1.0 - sig))).astype(BF16)
    refs[-1][...] = (grad_hidden * (gate * sig)).astype(BF16)


def finish(gate, up, terms, first, width, held, deps):
    tokens = gate.shape[0]
    window = pl.BlockSpec((pl.Element(tokens), pl.Element(width)), lambda i: (0, first))
    ins = [(gate, window), (up, window)]
    ins += [(t, pl.BlockSpec((1, width, tokens), lambda i: (0, 0, 0))) for t in terms]
    outs = [(gate.shape, BF16, window, x) for x in held]
    return run(finish_kernel, "finish", (1,), ins, outs, deps, exps=tokens * width)


def weight_grad_kernel(*refs):
    pieces, (source, out_ref, dy_ref, sems) = refs[:-4], refs[-4:]

    @pl.when(pl.program_id(0) == 0)
    def _():
        count = sems.shape[0]
        rows = dy_ref.shape[0] // count
        copies = []
        for n in range(count):
            cut = pl.ds(n * rows, rows)
            copies.append(pltpu.make_async_copy(source.at[cut], dy_ref.at[cut], sems.at[n]))
        for copy in copies:
            copy.start()
        for copy in copies:
            copy.wait()

    hidden = jnp.concatenate([ref[...] for ref in pieces], axis=1)
    out_ref[...] = jnp.dot(hidden, dy_ref[...], preferred_element_type=F32).astype(BF16)


def weight_grad(pieces, dy, whole, total, start, rows, deps):
    block = pieces[0][0].shape[1]
    tokens, depth = dy.shape
    tall = divisor(rows, 416, 16)

    def spec(base):
        return pl.BlockSpec((tall, block), lambda i: ((start - base) // tall + i, 0))

    ins = [(x, spec(base)) for x, base in pieces]
    ins.append((dy, pl.BlockSpec(memory_space=pl.ANY)))
    place = pl.BlockSpec((tall, depth), lambda i: (start // tall + i, 0))
    out = ((total, depth), BF16, place, whole)
    scratch = [pltpu.VMEM((tokens, depth), BF16), pltpu.SemaphoreType.DMA((8,))]
    flops = 2 * rows * tokens * depth
    return run(
        weight_grad_kernel, "weight_grad", (rows // tall,), ins, [out], deps, None, scratch, flops
    )[0]


def arrivals(z, count):
    found = []
    for s in range(1, count):
        if z - s >= 0:
            found.append(("up", s, z - s))
        if z + s < count:
            found.append(("down", s, z + s))
    return found


def pick(table, index):
    value = jnp.int32(table[0])
    for n in range(1, len(table)):
        value = jnp.where(index == n, jnp.int32(table[n]), value)
    return value


def program(row_count, col_count, grad_out, gate_act, up_act, down_weight):
    assert row_count == 2 * col_count
    row = lax.axis_index("row").astype(jnp.int32)
    col = lax.axis_index("col").astype(jnp.int32)
    core, chip = row % 2, row // 2
    bits = []
    while 2 ** (len(bits) + 1) < row_count:
        bits.append(2 ** (len(bits) + 1))
    streams = (bits, bits[::-1])
    width = down_weight.shape[0]
    block = gate_act.shape[0]
    tokens = row_count * block

    def swap(x, bit):
        pairs = [(r, r ^ bit) for r in range(row_count)]
        return jax.tree.map(lambda x: lax.ppermute(x, "row", pairs), x)

    places = []
    for order in streams:
        found = [0]
        for bit in order[::-1]:
            found = found + [f | bit // 2 for f in found]
        places.append([found.index(m) for m in range(row_count // 2)])

    ways = {"up": [grad_out], "down": [grad_out]}

    def forward(s):
        up, down = ways["up"], ways["down"]
        up.append(lax.ppermute(up[-1], "col", [(i, i + 1) for i in range(s - 1, col_count - 1)]))
        down.append(lax.ppermute(down[-1], "col", [(i, i - 1) for i in range(1, col_count - s + 1)]))

    def arrived(k):
        sources = [arrivals(z, col_count)[k - 1] for z in range(col_count)]
        kinds = sorted(set((way, s) for way, s, _ in sources))
        which = pick([kinds.index((way, s)) for way, s, _ in sources], col)
        return [ways[way][s] for way, s in kinds], which, pick([c for _, _, c in sources], col)

    units = width // LANES
    edges = [units * q // CHUNKS * LANES for q in range(CHUNKS + 1)]
    widths = [b - a for a, b in zip(edges, edges[1:])]
    terms = [(None, None)] * CHUNKS
    ordered = None

    def product(chunks, dy, deps):
        nonlocal ordered
        sources, which, place = dy
        flip = chip ^ place
        at = jnp.stack([pick(places[0], flip), core, 1 - core, flip, which, pick(places[1], flip)])
        first, last = chunks[0], chunks[-1] + 1
        out = hidden_grad_terms(
            at,
            sources,
            down_weight,
            edges[first],
            widths[first:last],
            terms[first:last],
            (ordered,) if first == 0 else None,
            tokens,
            deps,
        )
        for n, q in enumerate(chunks):
            terms[q] = (out[2 * n], out[2 * n + 1])
        if first == 0:
            ordered = out[-1]
        return out[0]

    forward(1)
    hidden = hidden_transposed(gate_act, up_act)
    held, base = {0: [hidden]}, {0: [0]}
    first_bits = bits[:2]
    for bit in first_bits + [1]:
        held[bit], base[bit] = swap([hidden], bit), [0]
    half = width // 2

    last = hidden
    dy = [grad_out], jnp.int32(0), col
    both = []
    for k in range(1, col_count):
        last = product(range(CHUNKS), dy, [last] + (held[1] if k == 2 else []))
        if k == 2 and len(first_bits) == 2:
            a, b = first_bits
            held[a], held[b], last = lax.optimization_barrier((held[a], held[b], last))
            both = [jnp.concatenate(held[a] + held[b])]
        ways["up"][k], ways["down"][k], last, both = lax.optimization_barrier(
            (ways["up"][k], ways["down"][k], last, both)
        )
        terms[0] = (last, terms[0][1])
        if k + 1 < col_count:
            forward(k + 1)
        dy = arrived(k)
        if k == 2 and len(first_bits) == 2:
            held[a | b] = [swap(held[a][0][:half], b), swap(held[b][0][half:], a)]
            base[a | b] = [0, half]
            held[a | 1] = held[b | 1] = swap(both, 1)
            base[a | 1], base[b | 1] = [0], [-width]

    held, last = lax.optimization_barrier((held, last))
    terms[0] = (last, terms[0][1])
    for bit in bits[2:]:
        for f in [f for f in held if f | bit not in held]:
            held[f | bit], base[f | bit] = swap(held[f], bit), base[f]
    ready = jax.tree.leaves(held)
    for f in [f for f in held if f | 1 not in held]:
        held[f | 1], base[f | 1] = swap(held[f], 1), base[f]

    grad_gate = grad_up = grad_down = None
    sums, stages = [None] * CHUNKS, [0] * CHUNKS

    def step(kind, n, last):
        nonlocal grad_gate, grad_up, grad_down
        if kind == "P":
            chunks = range(CHUNKS * n // GROUPS, CHUNKS * (n + 1) // GROUPS)
            deps = ready if n == 0 else jax.tree.leaves(held) if n == 1 else []
            last = product(chunks, dy, [last] + deps)
            for q in chunks:
                sums[q] = [terms[q][0], swap(terms[q][1], 1)]
            return last
        if kind == "S":
            bit = streams[n % 2][stages[n]]
            stages[n] += 1
            rows = (row_count // 2) >> stages[n]
            is_whole = last is grad_down
            sums[n], last = lax.optimization_barrier((sums[n], last))
            if is_whole:
                grad_down = last
            send = sum(t[rows : 2 * rows].astype(F32) for t in sums[n]).astype(BF16)
            sums[n] = sums[n] + [swap(send, bit)]
            return send
        if kind == "F":
            grad_gate, grad_up = finish(
                gate_act, up_act, sums[n], edges[n], widths[n], (grad_gate, grad_up), [last]
            )
            return grad_up
        start, stop = (width * x // 4 for x in PARTS[n])
        side = -1 if start >= half else 0
        pieces = [(held[f][side], base[f][side]) for f in range(row_count)]
        grad_down = weight_grad(pieces, ordered, grad_down, width, start, stop - start, [last])
        return grad_down

    for item in " ".join(PLAN).split():
        kind, n = item[0], int(item[1:])
        while kind == "F" and stages[n] < len(bits):
            last = step("S", n, last)
        last = step(kind, n, last)
    return grad_gate, grad_up, grad_down


def solution(mesh):
    def local(*args):
        return program(mesh.shape["row"], mesh.shape["col"], *args)

    return jax.shard_map(
        local,
        mesh=mesh,
        in_specs=(P("col", "row"), P("row", "col"), P("row", "col"), P("col", "row")),
        out_specs=(P("row", "col"), P("row", "col"), P("col", "row")),
        check_vma=False,
    )
```

```python
import functools
import math

import jax
import jax.numpy as jnp
from jax import lax
from jax.experimental import pallas as pl
from jax.experimental.pallas import tpu as pltpu
from jax.sharding import PartitionSpec as P

F32, BF16 = jnp.float32, jnp.bfloat16
VMEM_LIMIT = 63 * 1024 * 1024
CHUNKS = 4
GROUPS = 2
PARTS = [(0, 3), (3, 4)]
SPLIT = 4
LANES = 128
PLAN = ["P0 P1 S0 S1", "S2 S3 W0 S0", "S1 S2 S3 W1", "F0 F1 F2 F3"]


def divisor(extent, most, step):
    best = extent
    for size in range(step, most + 1, step):
        if extent % size == 0:
            best = size
    return best


def run(kernel, name, grid, ins, outs, deps=(), at=None, scratch=(), flops=0, exps=0):
    held = [(n, o[3]) for n, o in enumerate(outs) if o[3] is not None]
    deps = [d for d in deps if not any(d is x for _, x in held)]
    arrays = [x for x, _ in ins] + [x for _, x in held] + list(deps)
    specs = [s for _, s in ins] + [pl.BlockSpec(memory_space=pl.ANY)] * (len(held) + len(deps))
    lead = 0 if at is None else 1
    first_out = lead + len(arrays)

    def body(*refs):
        kernel(*refs[: lead + len(ins)], *refs[first_out:])

    moved = sum(x.size * x.dtype.itemsize for x, _ in ins)
    return pl.pallas_call(
        body,
        grid_spec=pltpu.PrefetchScalarGridSpec(
            num_scalar_prefetch=lead,
            grid=grid,
            in_specs=specs,
            out_specs=[o[2] for o in outs],
            scratch_shapes=scratch,
        ),
        out_shape=[jax.ShapeDtypeStruct(o[0], o[1]) for o in outs],
        input_output_aliases={lead + len(ins) + k: n for k, (n, _) in enumerate(held)},
        compiler_params=pltpu.CompilerParams(vmem_limit_bytes=VMEM_LIMIT),
        cost_estimate=pl.CostEstimate(
            flops=flops, bytes_accessed=moved, transcendentals=exps
        ),
        name=name,
    )(*([] if at is None else [at]), *arrays)


def hidden_kernel(gate_ref, up_ref, out_ref):
    gate = gate_ref[...].astype(F32)
    hidden = gate * jax.nn.sigmoid(gate) * up_ref[...].astype(F32)
    out_ref[...] = jnp.transpose(hidden.astype(BF16))


def hidden_transposed(gate, up):
    tokens, width = gate.shape
    step = divisor(width, 1664, 128)
    spec = pl.BlockSpec((tokens, step), lambda i: (0, i))
    out = ((width, tokens), BF16, pl.BlockSpec((step, tokens), lambda i: (i, 0)), None)
    return run(hidden_kernel, "hidden", (width // step,), [(gate, spec), (up, spec)], [out])[0]


def product_kernel(choices, counts, ordering, at_ref, *refs):
    weights, refs = refs[:SPLIT], refs[SPLIT:]
    sources, outs = refs[:choices], refs[choices:-4]
    dy_ref, turned_ref, sems, out_sem = refs[-4:]
    step = pl.program_id(0)
    block = dy_ref.shape[0] // 2
    to_order = None
    if ordering:
        place = outs[-1].at[pl.ds(pl.multiple_of(at_ref[3] * 2 * block, 2 * block), 2 * block)]
        to_order = pltpu.make_async_copy(dy_ref, place, out_sem)

    @pl.when(step == 0)
    def _():
        for n, source in enumerate(sources):

            @pl.when(at_ref[4] == n)
            def _():
                copies = []
                for side in range(2):
                    rows = pl.ds(pl.multiple_of(at_ref[1 + side] * block, block), block)
                    copies.append(
                        pltpu.make_async_copy(
                            source.at[rows], dy_ref.at[pl.ds(side * block, block)], sems.at[side]
                        )
                    )
                for copy in copies:
                    copy.start()
                for copy in copies:
                    copy.wait()

        if ordering:
            to_order.start()
        turned_ref[...] = jnp.transpose(dy_ref[...])

    turned = turned_ref[...]
    parts = [jnp.dot(ref[...], turned, preferred_element_type=F32) for ref in weights]
    rows = weights[0].shape[0]
    first = 0
    for q, count in enumerate(counts):

        @pl.when((step >= first) & (step < first + count))
        def _():
            for n, part in enumerate(parts):
                outs[2 * q][0, pl.ds(n * rows, rows)] = part[:, :block]
                outs[2 * q + 1][0, pl.ds(n * rows, rows)] = part[:, block:].astype(BF16)

        first += count

    if ordering:

        @pl.when(step == pl.num_programs(0) - 1)
        def _():
            to_order.wait()


def hidden_grad_terms(at, sources, weight, first, widths, held, ordered, total, deps):
    block, depth = sources[0].shape[0] // 2, sources[0].shape[1]
    tall = divisor(math.gcd(first, *widths), 832, 16 * SPLIT)
    counts = [w // tall for w in widths]

    def weight_spec(n):
        start = first // tall
        return pl.BlockSpec((tall // SPLIT, depth), lambda i, at: ((start + i) * SPLIT + n, 0))

    ins = [(weight, weight_spec(n)) for n in range(SPLIT)]
    ins += [(x, pl.BlockSpec(memory_space=pl.ANY)) for x in sources]
    outs, start = [], 0
    for q, (w, count) in enumerate(zip(widths, counts)):

        def place(i, at, where=0 if q % 2 == 0 else 5, start=start, count=count):
            return (at[where], jnp.clip(i - start, 0, count - 1), 0)

        spec = pl.BlockSpec((1, tall, block), place)
        shape = (total // (2 * block), w, block)
        outs += [(shape, F32, spec, held[q][0]), (shape, BF16, spec, held[q][1])]
        start += count
    if ordered is not None:
        outs.append(((total, depth), BF16, pl.BlockSpec(memory_space=pl.ANY), ordered[0]))
    kernel = functools.partial(product_kernel, len(sources), counts, ordered is not None)
    scratch = [
        pltpu.VMEM((2 * block, depth), BF16),
        pltpu.VMEM((depth, 2 * block), BF16),
        pltpu.SemaphoreType.DMA((2,)),
        pltpu.SemaphoreType.DMA,
    ]
    flops = 4 * block * depth * sum(widths)
    return run(
        kernel, "hidden_grad_terms", (start,), ins, outs, deps, at, scratch, flops
    )


def finish_kernel(gate_ref, up_ref, *refs):
    grad_hidden = jnp.transpose(sum(ref[0].astype(F32) for ref in refs[:-2]))
    gate, up = gate_ref[...].astype(F32), up_ref[...].astype(F32)
    sig = jax.nn.sigmoid(gate)
    refs[-2][...] = (grad_hidden * up * sig * (1.0 + gate * (1.0 - sig))).astype(BF16)
    refs[-1][...] = (grad_hidden * (gate * sig)).astype(BF16)


def finish(gate, up, terms, first, width, held, deps):
    tokens = gate.shape[0]
    window = pl.BlockSpec((pl.Element(tokens), pl.Element(width)), lambda i: (0, first))
    ins = [(gate, window), (up, window)]
    ins += [(t, pl.BlockSpec((1, width, tokens), lambda i: (0, 0, 0))) for t in terms]
    outs = [(gate.shape, BF16, window, x) for x in held]
    return run(finish_kernel, "finish", (1,), ins, outs, deps, exps=tokens * width)


def weight_grad_kernel(switch, shared, *refs):
    pieces, (source, out_ref, dy_ref, sems) = list(refs[:-4]), refs[-4:]

    @pl.when(pl.program_id(0) == 0)
    def _():
        count = sems.shape[0]
        rows = dy_ref.shape[0] // count
        copies = []
        for n in range(count):
            cut = pl.ds(n * rows, rows)
            copies.append(pltpu.make_async_copy(source.at[cut], dy_ref.at[cut], sems.at[n]))
        for copy in copies:
            copy.start()
        for copy in copies:
            copy.wait()

    blocks = []
    for count in shared:
        block = pieces.pop(0)[...]
        if count == 2:
            block = jnp.where(pl.program_id(0) < switch, block, pieces.pop(0)[...])
        blocks.append(block)
    hidden = jnp.concatenate(blocks, axis=1)
    out_ref[...] = jnp.dot(hidden, dy_ref[...], preferred_element_type=F32).astype(BF16)


def weight_grad(pieces, dy, whole, total, start, rows, deps):
    block = pieces[0][0][0].shape[1]
    tokens, depth = dy.shape
    middle = total // 2
    if start < middle < start + rows:
        tall = divisor(math.gcd(rows, middle - start), 416, 16)
        switch = (middle - start) // tall
    else:
        tall = divisor(rows, 416, 16)
        switch = 0
        pieces = [p if len(p) == 1 else [p[start >= middle]] for p in pieces]

    def spec(x, base):
        last = x.shape[0] // tall - 1
        return pl.BlockSpec(
            (tall, block), lambda i: (jnp.clip((start - base) // tall + i, 0, last), 0)
        )

    ins = [(x, spec(x, base)) for p in pieces for x, base in p]
    ins.append((dy, pl.BlockSpec(memory_space=pl.ANY)))
    place = pl.BlockSpec((tall, depth), lambda i: (start // tall + i, 0))
    out = ((total, depth), BF16, place, whole)
    scratch = [pltpu.VMEM((tokens, depth), BF16), pltpu.SemaphoreType.DMA((8,))]
    flops = 2 * rows * tokens * depth
    kernel = functools.partial(weight_grad_kernel, switch, [len(p) for p in pieces])
    return run(kernel, "weight_grad", (rows // tall,), ins, [out], deps, None, scratch, flops)[0]


def arrivals(z, count):
    found = []
    for s in range(1, count):
        if z - s >= 0:
            found.append(("up", s, z - s))
        if z + s < count:
            found.append(("down", s, z + s))
    return found


def pick(table, index):
    value = jnp.int32(table[0])
    for n in range(1, len(table)):
        value = jnp.where(index == n, jnp.int32(table[n]), value)
    return value


def program(row_count, col_count, grad_out, gate_act, up_act, down_weight):
    assert row_count == 2 * col_count
    row = lax.axis_index("row").astype(jnp.int32)
    col = lax.axis_index("col").astype(jnp.int32)
    core, chip = row % 2, row // 2
    bits = []
    while 2 ** (len(bits) + 1) < row_count:
        bits.append(2 ** (len(bits) + 1))
    streams = (bits, bits[::-1])
    width = down_weight.shape[0]
    block = gate_act.shape[0]
    tokens = row_count * block

    def swap(x, bit):
        pairs = [(r, r ^ bit) for r in range(row_count)]
        return jax.tree.map(lambda x: lax.ppermute(x, "row", pairs), x)

    places = []
    for order in streams:
        found = [0]
        for bit in order[::-1]:
            found = found + [f | bit // 2 for f in found]
        places.append([found.index(m) for m in range(row_count // 2)])

    ways = {"up": [grad_out], "down": [grad_out]}

    def forward(s):
        up, down = ways["up"], ways["down"]
        up.append(lax.ppermute(up[-1], "col", [(i, i + 1) for i in range(s - 1, col_count - 1)]))
        down.append(lax.ppermute(down[-1], "col", [(i, i - 1) for i in range(1, col_count - s + 1)]))

    def arrived(k):
        sources = [arrivals(z, col_count)[k - 1] for z in range(col_count)]
        kinds = sorted(set((way, s) for way, s, _ in sources))
        which = pick([kinds.index((way, s)) for way, s, _ in sources], col)
        return [ways[way][s] for way, s in kinds], which, pick([c for _, _, c in sources], col)

    units = width // LANES
    edges = [units * q // CHUNKS * LANES for q in range(CHUNKS + 1)]
    widths = [b - a for a, b in zip(edges, edges[1:])]
    terms = [(None, None)] * CHUNKS
    ordered = None

    def product(chunks, dy, deps):
        nonlocal ordered
        sources, which, place = dy
        flip = chip ^ place
        at = jnp.stack([pick(places[0], flip), core, 1 - core, flip, which, pick(places[1], flip)])
        first, last = chunks[0], chunks[-1] + 1
        out = hidden_grad_terms(
            at,
            sources,
            down_weight,
            edges[first],
            widths[first:last],
            terms[first:last],
            (ordered,) if first == 0 else None,
            tokens,
            deps,
        )
        for n, q in enumerate(chunks):
            terms[q] = (out[2 * n], out[2 * n + 1])
        if first == 0:
            ordered = out[-1]
        return out[0]

    forward(1)
    hidden = hidden_transposed(gate_act, up_act)
    held, base = {0: [hidden]}, {0: [0]}
    first_bits = bits[:2]
    for bit in first_bits + [1]:
        held[bit], base[bit] = swap([hidden], bit), [0]
    half = width // 2

    last = hidden
    dy = [grad_out], jnp.int32(0), col
    both = []
    for k in range(1, col_count):
        last = product(range(CHUNKS), dy, [last] + (held[1] if k == 2 else []))
        if k == 2 and len(first_bits) == 2:
            a, b = first_bits
            held[a], held[b], last = lax.optimization_barrier((held[a], held[b], last))
            both = [jnp.concatenate(held[a] + held[b])]
        ways["up"][k], ways["down"][k], last, both = lax.optimization_barrier(
            (ways["up"][k], ways["down"][k], last, both)
        )
        terms[0] = (last, terms[0][1])
        if k + 1 < col_count:
            forward(k + 1)
        dy = arrived(k)
        if k == 2 and len(first_bits) == 2:
            held[a | b] = [swap(held[a][0][:half], b), swap(held[b][0][half:], a)]
            base[a | b] = [0, half]
            held[a | 1] = held[b | 1] = swap(both, 1)
            base[a | 1], base[b | 1] = [0], [-width]

    held, last = lax.optimization_barrier((held, last))
    terms[0] = (last, terms[0][1])
    for bit in bits[2:]:
        for f in [f for f in held if f | bit not in held]:
            held[f | bit], base[f | bit] = swap(held[f], bit), base[f]
    ready = jax.tree.leaves(held)
    for f in [f for f in held if f | 1 not in held]:
        held[f | 1], base[f | 1] = swap(held[f], 1), base[f]

    grad_gate = grad_up = grad_down = None
    sums, stages = [None] * CHUNKS, [0] * CHUNKS

    def step(kind, n, last):
        nonlocal grad_gate, grad_up, grad_down
        if kind == "P":
            chunks = range(CHUNKS * n // GROUPS, CHUNKS * (n + 1) // GROUPS)
            deps = ready if n == 0 else jax.tree.leaves(held) if n == 1 else []
            last = product(chunks, dy, [last] + deps)
            for q in chunks:
                sums[q] = [terms[q][0], swap(terms[q][1], 1)]
            return last
        if kind == "S":
            bit = streams[n % 2][stages[n]]
            stages[n] += 1
            rows = (row_count // 2) >> stages[n]
            is_whole = last is grad_down
            sums[n], last = lax.optimization_barrier((sums[n], last))
            if is_whole:
                grad_down = last
            send = sum(t[rows : 2 * rows].astype(F32) for t in sums[n]).astype(BF16)
            sums[n] = sums[n] + [swap(send, bit)]
            return send
        if kind == "F":
            grad_gate, grad_up = finish(
                gate_act, up_act, sums[n], edges[n], widths[n], (grad_gate, grad_up), [last]
            )
            return grad_up
        start, stop = (width * x // 4 for x in PARTS[n])
        pieces = [list(zip(held[f], base[f])) for f in range(row_count)]
        grad_down = weight_grad(pieces, ordered, grad_down, width, start, stop - start, [last])
        return grad_down

    for item in " ".join(PLAN).split():
        kind, n = item[0], int(item[1:])
        while kind == "F" and stages[n] < len(bits):
            last = step("S", n, last)
        last = step(kind, n, last)
    return grad_gate, grad_up, grad_down


def solution(mesh):
    def local(*args):
        return program(mesh.shape["row"], mesh.shape["col"], *args)

    return jax.shard_map(
        local,
        mesh=mesh,
        in_specs=(P("col", "row"), P("row", "col"), P("row", "col"), P("col", "row")),
        out_specs=(P("row", "col"), P("row", "col"), P("col", "row")),
        check_vma=False,
    )
```

```python
import functools
import math

import jax
import jax.numpy as jnp
from jax import lax
from jax.experimental import pallas as pl
from jax.experimental.pallas import tpu as pltpu
from jax.sharding import PartitionSpec as P

F32, BF16 = jnp.float32, jnp.bfloat16
VMEM_LIMIT = 63 * 1024 * 1024
CHUNKS = 4
GROUPS = 2
PARTS = [(0, 3), (3, 4)]
SPLIT = 4
LANES = 128
PLAN = ["P0 P1 S0 S1", "S2 S3 W0 S0", "S1 S2 S3 W1", "F0 F1 F2 F3"]


def divisor(extent, most, step):
    best = extent
    for size in range(step, most + 1, step):
        if extent % size == 0:
            best = size
    return best


def run(kernel, name, grid, ins, outs, deps=(), at=None, scratch=(), flops=0, exps=0):
    held = [(n, o[3]) for n, o in enumerate(outs) if o[3] is not None]
    deps = [d for d in deps if not any(d is x for _, x in held)]
    arrays = [x for x, _ in ins] + [x for _, x in held] + list(deps)
    specs = [s for _, s in ins] + [pl.BlockSpec(memory_space=pl.ANY)] * (len(held) + len(deps))
    lead = 0 if at is None else 1
    first_out = lead + len(arrays)

    def body(*refs):
        kernel(*refs[: lead + len(ins)], *refs[first_out:])

    moved = sum(x.size * x.dtype.itemsize for x, _ in ins)
    return pl.pallas_call(
        body,
        grid_spec=pltpu.PrefetchScalarGridSpec(
            num_scalar_prefetch=lead,
            grid=grid,
            in_specs=specs,
            out_specs=[o[2] for o in outs],
            scratch_shapes=scratch,
        ),
        out_shape=[jax.ShapeDtypeStruct(o[0], o[1]) for o in outs],
        input_output_aliases={lead + len(ins) + k: n for k, (n, _) in enumerate(held)},
        compiler_params=pltpu.CompilerParams(vmem_limit_bytes=VMEM_LIMIT),
        cost_estimate=pl.CostEstimate(
            flops=flops, bytes_accessed=moved, transcendentals=exps
        ),
        name=name,
    )(*([] if at is None else [at]), *arrays)


def hidden_kernel(gate_ref, up_ref, out_ref):
    gate = gate_ref[...].astype(F32)
    hidden = gate * jax.nn.sigmoid(gate) * up_ref[...].astype(F32)
    out_ref[...] = jnp.transpose(hidden.astype(BF16))


def hidden_transposed(gate, up):
    tokens, width = gate.shape
    step = divisor(width, 1664, 128)
    spec = pl.BlockSpec((tokens, step), lambda i: (0, i))
    out = ((width, tokens), BF16, pl.BlockSpec((step, tokens), lambda i: (i, 0)), None)
    return run(hidden_kernel, "hidden", (width // step,), [(gate, spec), (up, spec)], [out])[0]


def product_kernel(choices, counts, ordering, at_ref, *refs):
    weights, refs = refs[:SPLIT], refs[SPLIT:]
    sources, outs = refs[:choices], refs[choices:-4]
    dy_ref, turned_ref, sems, out_sem = refs[-4:]
    step = pl.program_id(0)
    block = dy_ref.shape[0] // 2
    to_order = None
    if ordering:
        place = outs[-1].at[pl.ds(pl.multiple_of(at_ref[3] * 2 * block, 2 * block), 2 * block)]
        to_order = pltpu.make_async_copy(dy_ref, place, out_sem)

    @pl.when(step == 0)
    def _():
        for n, source in enumerate(sources):

            @pl.when(at_ref[4] == n)
            def _():
                copies = []
                for side in range(2):
                    rows = pl.ds(pl.multiple_of(at_ref[1 + side] * block, block), block)
                    copies.append(
                        pltpu.make_async_copy(
                            source.at[rows], dy_ref.at[pl.ds(side * block, block)], sems.at[side]
                        )
                    )
                for copy in copies:
                    copy.start()
                for copy in copies:
                    copy.wait()

        if ordering:
            to_order.start()
        turned_ref[...] = jnp.transpose(dy_ref[...])

    turned = turned_ref[...]
    parts = [jnp.dot(ref[...], turned, preferred_element_type=F32) for ref in weights]
    rows = weights[0].shape[0]
    first = 0
    for q, count in enumerate(counts):

        @pl.when((step >= first) & (step < first + count))
        def _():
            for n, part in enumerate(parts):
                outs[2 * q][0, pl.ds(n * rows, rows)] = part[:, :block]
                outs[2 * q + 1][0, pl.ds(n * rows, rows)] = part[:, block:].astype(BF16)

        first += count

    if ordering:

        @pl.when(step == pl.num_programs(0) - 1)
        def _():
            to_order.wait()


def hidden_grad_terms(at, sources, weight, first, widths, held, ordered, total, deps):
    block, depth = sources[0].shape[0] // 2, sources[0].shape[1]
    tall = divisor(math.gcd(first, *widths), 832, 16 * SPLIT)
    counts = [w // tall for w in widths]

    def weight_spec(n):
        start = first // tall
        return pl.BlockSpec((tall // SPLIT, depth), lambda i, at: ((start + i) * SPLIT + n, 0))

    ins = [(weight, weight_spec(n)) for n in range(SPLIT)]
    ins += [(x, pl.BlockSpec(memory_space=pl.ANY)) for x in sources]
    outs, start = [], 0
    for q, (w, count) in enumerate(zip(widths, counts)):

        def place(i, at, where=0 if q % 2 == 0 else 5, start=start, count=count):
            return (at[where], jnp.clip(i - start, 0, count - 1), 0)

        spec = pl.BlockSpec((1, tall, block), place)
        shape = (total // (2 * block), w, block)
        outs += [(shape, F32, spec, held[q][0]), (shape, BF16, spec, held[q][1])]
        start += count
    if ordered is not None:
        outs.append(((total, depth), BF16, pl.BlockSpec(memory_space=pl.ANY), ordered[0]))
    kernel = functools.partial(product_kernel, len(sources), counts, ordered is not None)
    scratch = [
        pltpu.VMEM((2 * block, depth), BF16),
        pltpu.VMEM((depth, 2 * block), BF16),
        pltpu.SemaphoreType.DMA((2,)),
        pltpu.SemaphoreType.DMA,
    ]
    flops = 4 * block * depth * sum(widths)
    return run(
        kernel, "hidden_grad_terms", (start,), ins, outs, deps, at, scratch, flops
    )


def finish_kernel(gate_ref, up_ref, *refs):
    grad_hidden = jnp.transpose(sum(ref[0].astype(F32) for ref in refs[:-2]))
    gate, up = gate_ref[...].astype(F32), up_ref[...].astype(F32)
    sig = jax.nn.sigmoid(gate)
    refs[-2][...] = (grad_hidden * up * sig * (1.0 + gate * (1.0 - sig))).astype(BF16)
    refs[-1][...] = (grad_hidden * (gate * sig)).astype(BF16)


def finish(gate, up, terms, first, width, held, deps):
    tokens = gate.shape[0]
    window = pl.BlockSpec((pl.Element(tokens), pl.Element(width)), lambda i: (0, first))
    ins = [(gate, window), (up, window)]
    ins += [(t, pl.BlockSpec((1, width, tokens), lambda i: (0, 0, 0))) for t in terms]
    outs = [(gate.shape, BF16, window, x) for x in held]
    return run(finish_kernel, "finish", (1,), ins, outs, deps, exps=tokens * width)


def weight_grad_kernel(switch, shared, *refs):
    pieces, (source, out_ref, dy_ref, sems) = list(refs[:-4]), refs[-4:]

    @pl.when(pl.program_id(0) == 0)
    def _():
        count = sems.shape[0]
        rows = dy_ref.shape[0] // count
        copies = []
        for n in range(count):
            cut = pl.ds(n * rows, rows)
            copies.append(pltpu.make_async_copy(source.at[cut], dy_ref.at[cut], sems.at[n]))
        for copy in copies:
            copy.start()
        for copy in copies:
            copy.wait()

    blocks = []
    for count in shared:
        block = pieces.pop(0)[...]
        if count == 2:
            block = jnp.where(pl.program_id(0) < switch, block, pieces.pop(0)[...])
        blocks.append(block)
    hidden = jnp.concatenate(blocks, axis=1)
    out_ref[...] = jnp.dot(hidden, dy_ref[...], preferred_element_type=F32).astype(BF16)


def weight_grad(pieces, dy, whole, total, start, rows, deps):
    block = pieces[0][0][0].shape[1]
    tokens, depth = dy.shape
    middle = total // 2
    if start < middle < start + rows:
        tall = divisor(math.gcd(rows, middle - start), 832, 16)
        switch = (middle - start) // tall
    else:
        tall = divisor(rows, 832, 16)
        switch = 0
        pieces = [p if len(p) == 1 else [p[start >= middle]] for p in pieces]

    def spec(x, base):
        last = x.shape[0] // tall - 1
        return pl.BlockSpec(
            (tall, block), lambda i: (jnp.clip((start - base) // tall + i, 0, last), 0)
        )

    ins = [(x, spec(x, base)) for p in pieces for x, base in p]
    ins.append((dy, pl.BlockSpec(memory_space=pl.ANY)))
    place = pl.BlockSpec((tall, depth), lambda i: (start // tall + i, 0))
    out = ((total, depth), BF16, place, whole)
    scratch = [pltpu.VMEM((tokens, depth), BF16), pltpu.SemaphoreType.DMA((8,))]
    flops = 2 * rows * tokens * depth
    kernel = functools.partial(weight_grad_kernel, switch, [len(p) for p in pieces])
    return run(kernel, "weight_grad", (rows // tall,), ins, [out], deps, None, scratch, flops)[0]


def arrivals(z, count):
    found = []
    for s in range(1, count):
        if z - s >= 0:
            found.append(("up", s, z - s))
        if z + s < count:
            found.append(("down", s, z + s))
    return found


def pick(table, index):
    value = jnp.int32(table[0])
    for n in range(1, len(table)):
        value = jnp.where(index == n, jnp.int32(table[n]), value)
    return value


def program(row_count, col_count, grad_out, gate_act, up_act, down_weight):
    assert row_count == 2 * col_count
    row = lax.axis_index("row").astype(jnp.int32)
    col = lax.axis_index("col").astype(jnp.int32)
    core, chip = row % 2, row // 2
    bits = []
    while 2 ** (len(bits) + 1) < row_count:
        bits.append(2 ** (len(bits) + 1))
    streams = (bits, bits[::-1])
    width = down_weight.shape[0]
    block = gate_act.shape[0]
    tokens = row_count * block

    def swap(x, bit):
        pairs = [(r, r ^ bit) for r in range(row_count)]
        return jax.tree.map(lambda x: lax.ppermute(x, "row", pairs), x)

    places = []
    for order in streams:
        found = [0]
        for bit in order[::-1]:
            found = found + [f | bit // 2 for f in found]
        places.append([found.index(m) for m in range(row_count // 2)])

    ways = {"up": [grad_out], "down": [grad_out]}

    def forward(s):
        up, down = ways["up"], ways["down"]
        up.append(lax.ppermute(up[-1], "col", [(i, i + 1) for i in range(s - 1, col_count - 1)]))
        down.append(lax.ppermute(down[-1], "col", [(i, i - 1) for i in range(1, col_count - s + 1)]))

    def arrived(k):
        sources = [arrivals(z, col_count)[k - 1] for z in range(col_count)]
        kinds = sorted(set((way, s) for way, s, _ in sources))
        which = pick([kinds.index((way, s)) for way, s, _ in sources], col)
        return [ways[way][s] for way, s in kinds], which, pick([c for _, _, c in sources], col)

    units = width // LANES
    edges = [units * q // CHUNKS * LANES for q in range(CHUNKS + 1)]
    widths = [b - a for a, b in zip(edges, edges[1:])]
    terms = [(None, None)] * CHUNKS
    ordered = None

    def product(chunks, dy, deps):
        nonlocal ordered
        sources, which, place = dy
        flip = chip ^ place
        at = jnp.stack([pick(places[0], flip), core, 1 - core, flip, which, pick(places[1], flip)])
        first, last = chunks[0], chunks[-1] + 1
        out = hidden_grad_terms(
            at,
            sources,
            down_weight,
            edges[first],
            widths[first:last],
            terms[first:last],
            (ordered,) if first == 0 else None,
            tokens,
            deps,
        )
        for n, q in enumerate(chunks):
            terms[q] = (out[2 * n], out[2 * n + 1])
        if first == 0:
            ordered = out[-1]
        return out[0]

    forward(1)
    hidden = hidden_transposed(gate_act, up_act)
    held, base = {0: [hidden]}, {0: [0]}
    first_bits = bits[:2]
    for bit in first_bits + [1]:
        held[bit], base[bit] = swap([hidden], bit), [0]
    half = width // 2

    last = hidden
    dy = [grad_out], jnp.int32(0), col
    both = []
    for k in range(1, col_count):
        last = product(range(CHUNKS), dy, [last] + (held[1] if k == 2 else []))
        if k == 2 and len(first_bits) == 2:
            a, b = first_bits
            held[a], held[b], last = lax.optimization_barrier((held[a], held[b], last))
            both = [jnp.concatenate(held[a] + held[b])]
        ways["up"][k], ways["down"][k], last, both = lax.optimization_barrier(
            (ways["up"][k], ways["down"][k], last, both)
        )
        terms[0] = (last, terms[0][1])
        if k + 1 < col_count:
            forward(k + 1)
        dy = arrived(k)
        if k == 2 and len(first_bits) == 2:
            held[a | b] = [swap(held[a][0][:half], b), swap(held[b][0][half:], a)]
            base[a | b] = [0, half]
            held[a | 1] = held[b | 1] = swap(both, 1)
            base[a | 1], base[b | 1] = [0], [-width]

    held, last = lax.optimization_barrier((held, last))
    terms[0] = (last, terms[0][1])
    for bit in bits[2:]:
        for f in [f for f in held if f | bit not in held]:
            held[f | bit], base[f | bit] = swap(held[f], bit), base[f]
    ready = jax.tree.leaves(held)
    for f in [f for f in held if f | 1 not in held]:
        held[f | 1], base[f | 1] = swap(held[f], 1), base[f]

    grad_gate = grad_up = grad_down = None
    sums, stages = [None] * CHUNKS, [0] * CHUNKS

    def step(kind, n, last):
        nonlocal grad_gate, grad_up, grad_down
        if kind == "P":
            chunks = range(CHUNKS * n // GROUPS, CHUNKS * (n + 1) // GROUPS)
            deps = ready if n == 0 else jax.tree.leaves(held) if n == 1 else []
            last = product(chunks, dy, [last] + deps)
            for q in chunks:
                sums[q] = [terms[q][0], swap(terms[q][1], 1)]
            return last
        if kind == "S":
            bit = streams[n % 2][stages[n]]
            stages[n] += 1
            rows = (row_count // 2) >> stages[n]
            is_whole = last is grad_down
            sums[n], last = lax.optimization_barrier((sums[n], last))
            if is_whole:
                grad_down = last
            send = sum(t[rows : 2 * rows].astype(F32) for t in sums[n]).astype(BF16)
            sums[n] = sums[n] + [swap(send, bit)]
            return send
        if kind == "F":
            grad_gate, grad_up = finish(
                gate_act, up_act, sums[n], edges[n], widths[n], (grad_gate, grad_up), [last]
            )
            return grad_up
        start, stop = (width * x // 4 for x in PARTS[n])
        pieces = [list(zip(held[f], base[f])) for f in range(row_count)]
        grad_down = weight_grad(pieces, ordered, grad_down, width, start, stop - start, [last])
        return grad_down

    for item in " ".join(PLAN).split():
        kind, n = item[0], int(item[1:])
        while kind == "F" and stages[n] < len(bits):
            last = step("S", n, last)
        last = step(kind, n, last)
    return grad_gate, grad_up, grad_down


def solution(mesh):
    def local(*args):
        return program(mesh.shape["row"], mesh.shape["col"], *args)

    return jax.shard_map(
        local,
        mesh=mesh,
        in_specs=(P("col", "row"), P("row", "col"), P("row", "col"), P("col", "row")),
        out_specs=(P("row", "col"), P("row", "col"), P("col", "row")),
        check_vma=False,
    )
```
